128 devices in a mesh: prow: 8 (over y, core), pcol: 16 (over z, x).
Axes of the slice: x: 4, y: 4, z: 4, core: 2. Of those that a mesh axis runs over, the one named last changes fastest.
Arguments:
- omega: bfloat16 [320, 2, 131072], P(None, None, ('prow', 'pcol')), may hold values from -6 to 6
- u_basis: bfloat16 [2, 131072, 1024], P(None, ('prow', 'pcol')), may hold values from -0.1875 to 0.1875
- v_basis: bfloat16 [2, 131072, 1024], P(None, ('prow', 'pcol')), may hold values from -0.015625 to 0.015625
- coupling: bfloat16 [2, 1024, 1024], replicated, may hold values from -0.1875 to 0.1875
- leaf_blocks: bfloat16 [2, 512, 256, 256], P(None, ('prow', 'pcol')), may hold values from -0.375 to 0.375
- child_map: int32 [2, 1024], P(None, ('prow', 'pcol')), may hold values from 0 to 2047, as said below
Outputs:
- parent_y: float32 [2048, 320, 128], P('prow', 'pcol')
- parent_z: float32 [2048, 320, 128], P('prow', 'pcol')
The draws below stay inside these ranges and needn't reach their ends.
Inputs may be any that keep to these rules, and one draw needn't show every extreme that they name: `child_map`: parent block q belongs to process row q // 256. The blocks of one child go to distinct parent blocks. Process row p holds blocks p * 128 to (p + 1) * 128 - 1 of each child; of the 256 child blocks that one process row holds, at most 64 go to the parent blocks of one process row, and in every draw some process row receives exactly 64 from every process row.
All inputs are finite; a program needn't handle non-finite values.
Results may differ from the reference program's by a relative error of at most 0.006.
Values may be sent and summed in bfloat16 or wider, within the bound.
No kernel may reach another device: no remote copies, remote signals or barrier semaphores. Data moves between devices by JAX's collectives and lax.ppermute only.
A program may use at most 128 MiB of HBM per device.

```python
import jax
import jax.numpy as jnp
from jax import lax

BLK = 128
LEAF = 256
R = 1024
S = 320
NBC = 1024
NC = 131072
NPB = 2048
PBR = 256
CAP = 64


def draw_child_map(key, part):
    key = jax.random.fold_in(key, 11)
    row_count = NPB // PBR
    half_len = PBR // 2
    half_cap = CAP // 2
    heavy = jax.random.randint(jax.random.fold_in(key, 1), (), 0, row_count)
    position = jnp.arange(half_len)
    others = (heavy + 1 + jnp.mod(position - half_cap, row_count - 1)) % row_count
    sequence = jnp.where(position < half_cap, heavy, others)
    source_keys = jax.random.split(jax.random.fold_in(key, 2), 2 * row_count)
    shuffles = jax.vmap(lambda one_key: jax.random.permutation(one_key, half_len))(source_keys)
    targets_row = sequence[shuffles].reshape(2, NBC)
    row_hits = (targets_row[:, :, None] == jnp.arange(row_count)[None, None, :]).astype(jnp.int32)
    earlier = jnp.cumsum(row_hits, axis=1) - row_hits
    order = jnp.sum(earlier * row_hits, axis=2)
    owner_keys = jax.random.split(jax.random.fold_in(key, 3), 2 * row_count)
    placements = jax.vmap(lambda one_key: jax.random.permutation(one_key, PBR))(owner_keys).reshape(2, row_count, PBR)
    local_block = placements[jnp.arange(2)[:, None], targets_row, order]
    return (targets_row * PBR + local_block).astype(jnp.int32)


def level_of(rng, dims, cuts, low, top_value):
    def one(dim, blocks):
        draws = jax.random.uniform(jax.random.fold_in(jax.random.fold_in(rng, 6), dim), (blocks,), jnp.float32, low / len(cuts), top_value / len(cuts))
        return jnp.repeat(jnp.exp(draws), dims[dim] // blocks).reshape((-1,) + (1,) * (len(dims) - dim - 1))

    level = one(*cuts[0])
    for cut in cuts[1:]:
        level = level * one(*cut)
    return level


def bell_draw(key, shape, scale, bound, shards=(), dtype=jnp.bfloat16):
    drawn = jax.random.normal(key, shape, jnp.float32) * scale
    if len(shards) > 0:
        drawn = level_of(key, shape, shards, -0.22, 0.18) * drawn
    return jnp.clip(drawn, min=-bound, max=bound).astype(dtype)


def setup_inputs(seed: int = 0) -> dict:
    arg_keys = jax.random.split(jax.random.key(seed), 7)
    omega = bell_draw(arg_keys[0], (S, 2, NC), 1.0, 6.0, ((2, 128),))
    u_basis = bell_draw(arg_keys[1], (2, NC, R), R ** -0.5, 0.1875, ((1, 128),))
    v_basis = bell_draw(arg_keys[2], (2, NC, R), NC ** -0.5, 0.015625, ((1, 128),))
    coupling = bell_draw(arg_keys[3], (2, R, R), R ** -0.5, 0.1875)
    leaf_blocks = bell_draw(arg_keys[4], (2, NC // LEAF, LEAF, LEAF), LEAF ** -0.5, 0.375, ((1, 128),))
    child_map = draw_child_map(jax.random.fold_in(arg_keys[6], 71), 0)
    return dict(omega=omega, u_basis=u_basis, v_basis=v_basis, coupling=coupling, leaf_blocks=leaf_blocks, child_map=child_map)


def child_samples(omega, u_basis, v_basis, coupling, leaf_blocks, child_id):
    probes = omega[:, child_id, :]
    u_rows = u_basis[child_id]
    v_rows = v_basis[child_id]
    contract_last = (((1,), (1,)), ((), ()))
    v_probe = jnp.dot(probes, v_rows, preferred_element_type=jnp.float32).astype(jnp.bfloat16)
    u_probe = jnp.dot(probes, u_rows, preferred_element_type=jnp.float32).astype(jnp.bfloat16)
    coupled = coupling[child_id]
    y_inner = lax.dot_general(v_probe, coupled, contract_last, preferred_element_type=jnp.float32).astype(jnp.bfloat16)
    z_inner = jnp.dot(u_probe, coupled, preferred_element_type=jnp.float32).astype(jnp.bfloat16)
    y_low = lax.dot_general(y_inner, u_rows, contract_last, preferred_element_type=jnp.float32)
    z_low = lax.dot_general(z_inner, v_rows, contract_last, preferred_element_type=jnp.float32)
    leaf_count = NC // LEAF
    leaves = leaf_blocks[child_id].astype(jnp.float32)
    grid = probes.astype(jnp.float32).reshape(S, leaf_count, LEAF)
    y_leaf = jnp.einsum('slk,lik->sli', grid, leaves)
    z_leaf = jnp.einsum('sli,lik->slk', grid, leaves)
    y_samp = (y_low + y_leaf.reshape(S, NC)).astype(jnp.bfloat16)
    z_samp = (z_low + z_leaf.reshape(S, NC)).astype(jnp.bfloat16)
    return y_samp, z_samp


def reference(omega, u_basis, v_basis, coupling, leaf_blocks, child_map):
    parent_y = jnp.zeros((NPB, S, BLK), jnp.float32)
    parent_z = jnp.zeros((NPB, S, BLK), jnp.float32)
    for child_id in range(2):
        y_samp, z_samp = child_samples(omega, u_basis, v_basis, coupling, leaf_blocks, child_id)
        targets = child_map[child_id]
        y_blocks = jnp.transpose(y_samp.reshape(S, NBC, BLK), (1, 0, 2)).astype(jnp.float32)
        right_sample_blocks = jnp.transpose(z_samp.reshape(S, NBC, BLK), (1, 0, 2)).astype(jnp.float32)
        parent_y = parent_y.at[targets].add(y_blocks)
        parent_z = parent_z.at[targets].add(right_sample_blocks)
    return parent_y, parent_z
```

```python
import functools

import jax
import jax.numpy as jnp
from jax import lax
from jax.experimental import pallas as pl
from jax.experimental.pallas import tpu as pltpu
from jax.sharding import Mesh, PartitionSpec as P

BLK = 128
ALL = ("y", "core", "z", "x")
RING = 4
STEPS = (1, 3, 2)
INFO = 8
BF16, F32 = jnp.bfloat16, jnp.float32


def ring_y(x, step):
    return lax.ppermute(x, "y", [(i, (i + step) % RING) for i in range(RING)])


def swap_core(x):
    return lax.ppermute(x, "core", [(0, 1), (1, 0)])


def ring_zx(x, first, step):
    pairs = []
    for core in range(2):
        for zz in range(RING):
            for xx in range(RING):
                along_x = (core == 0) == first
                to_z = zz if along_x else (zz + step) % RING
                to_x = (xx + step) % RING if along_x else xx
                pairs.append(((core * RING + zz) * RING + xx, (core * RING + to_z) * RING + to_x))
    return lax.ppermute(x, ("core", "z", "x"), pairs)


VMEM = pl.BlockSpec(memory_space=pltpu.VMEM)
SMEM = pl.BlockSpec(memory_space=pltpu.SMEM)
HBM = pl.BlockSpec(memory_space=pl.ANY)


def params(mib):
    return pltpu.CompilerParams(vmem_limit_bytes=mib * 2**20)


def pick_kernel(place, v_own, v_got, u_own, u_got, *rest):
    outs, (own, got, sems) = rest[:RING], rest[RING:]
    me, core = place[0], place[1]

    def copies(first, second, k):
        at = lax.rem(me + k, RING)
        return (
            pltpu.make_async_copy(first.at[at], own.at[k], sems.at[0, k]),
            pltpu.make_async_copy(second.at[at], got.at[k], sems.at[1, k]),
        )

    order = (1, 3, 2, 0)

    @pl.when(core == 0)
    def _():
        for k in order:
            for copy in copies(v_own, v_got, k):
                copy.start()

    @pl.when(core == 1)
    def _():
        for k in order:
            for copy in copies(u_own, u_got, k):
                copy.start()

    for k in order:
        for copy in copies(v_own, v_got, k):
            copy.wait()
        outs[k][...] = (own[k].astype(F32) + got[k].astype(F32)).astype(BF16)


def pick(place, *parts):
    _, rows, rank = parts[0].shape
    return pl.pallas_call(
        pick_kernel,
        out_shape=[jax.ShapeDtypeStruct((rows, rank), BF16)] * RING,
        in_specs=[SMEM] + [HBM] * 4,
        out_specs=[VMEM] * RING,
        scratch_shapes=[
            pltpu.VMEM((RING, rows, rank), BF16),
            pltpu.VMEM((RING, rows, rank), BF16),
            pltpu.SemaphoreType.DMA((2, RING)),
        ],
        compiler_params=params(16),
    )(place, *parts)


def sum_split_kernel(place, *refs):
    ins, outs = refs[:RING], refs[RING:]
    for k in range(RING):
        at = lax.rem(place[0] + k, RING)
        total = ins[0][at].astype(F32)
        for part in ins[1:]:
            total = total + part[at].astype(F32)
        outs[k][...] = total.astype(BF16)


def sum_split(place, parts):
    rows, rank = parts[0].shape
    shaped = [p.reshape(RING, rows // RING, rank) for p in parts]
    return pl.pallas_call(
        sum_split_kernel,
        out_shape=[jax.ShapeDtypeStruct((rows // RING, rank), BF16)] * RING,
        in_specs=[SMEM] + [VMEM] * RING,
        out_specs=[VMEM] * RING,
        compiler_params=params(16),
    )(place, *shaped)


def sum_info_kernel(a, b, c, d, info, out):
    total = a[...].astype(F32) + b[...].astype(F32) + c[...].astype(F32) + d[...].astype(F32)
    out[...] = jnp.concatenate([total, info[...]], axis=0).astype(BF16)


def sum_info(parts, info):
    rows, rank = parts[0].shape
    return pl.pallas_call(
        sum_info_kernel,
        out_shape=jax.ShapeDtypeStruct((rows + INFO, rank), BF16),
        in_specs=[VMEM] * 5,
        out_specs=VMEM,
        compiler_params=params(16),
    )(*parts, info)


def couple_kernel(a, b, c, d, weight, out):
    parts = [r[...].astype(F32) for r in (a, b, c, d)]
    rows = out.shape[0] - INFO
    probe = (parts[0] + parts[1] + parts[2] + parts[3]).astype(BF16)
    inner = jnp.dot(probe, weight[...], preferred_element_type=F32)
    infos = [p[rows : rows + 1] for p in parts] + [jnp.zeros((INFO - RING, out.shape[1]), F32)]
    out[...] = jnp.concatenate([inner[:rows]] + infos, axis=0).astype(BF16)


def couple(parts, weight):
    return pl.pallas_call(
        couple_kernel,
        out_shape=jax.ShapeDtypeStruct(parts[0].shape, BF16),
        in_specs=[VMEM] * 5,
        out_specs=VMEM,
        compiler_params=params(16),
    )(*parts, weight)


def expand_kernel(flip, place, *refs):
    held, (basis, probes, leaf, out, lhs, sems) = refs[: 2 * RING], refs[2 * RING :]
    a_me, b_me, own = place[0], place[1], place[2]
    child, tile = pl.program_id(0), pl.program_id(1)

    def copies(side):
        for j in range(RING):
            for m in range(RING):
                to = lhs.at[lax.rem(a_me + RING - j, RING), lax.rem(b_me + RING - m, RING)]
                yield pltpu.make_async_copy(held[side * RING + j].at[m], to, sems.at[j, m])

    @pl.when((child == 0) & (tile == 0))
    def _():
        @pl.when(own == 1)
        def _():
            for copy in copies(0):
                copy.start()

        @pl.when(own == 0)
        def _():
            for copy in copies(1):
                copy.start()

        for copy in copies(0):
            copy.wait()

    rows = lhs.shape[2] - INFO
    rank = lhs.shape[3]
    left = lhs[pl.ds(2 * child, 2)].reshape(-1, rank)
    low = lax.dot_general(left, basis[0], (((1,), (1,)), ((), ())), preferred_element_type=F32)
    low = jnp.concatenate([low[i : i + rows] for i in range(0, low.shape[0], rows + INFO)], axis=0)
    side = 1 if flip else 0
    near = lax.dot_general(probes[...], leaf[0, 0], (((1,), (side,)), ((), ())), preferred_element_type=F32)
    out[0] = (low + near).astype(BF16)


def expand(place, held, basis, probes, leaf_blocks, flip):
    _, local, rank = basis.shape
    samples = probes.shape[0]
    leaf = leaf_blocks.shape[2]
    tiles = local // leaf
    rows = held[0].shape[1]
    return pl.pallas_call(
        functools.partial(expand_kernel, flip),
        grid=(2, tiles),
        out_shape=jax.ShapeDtypeStruct((2, samples, local), BF16),
        in_specs=[SMEM]
        + [HBM] * (2 * RING)
        + [
            pl.BlockSpec((1, leaf, rank), lambda c, t: (c, t, 0)),
            pl.BlockSpec((samples, leaf), lambda c, t: (0, c * tiles + t)),
            pl.BlockSpec((1, 1, leaf, leaf), lambda c, t: (c, t, 0, 0)),
        ],
        out_specs=pl.BlockSpec((1, samples, leaf), lambda c, t: (c, 0, t)),
        scratch_shapes=[
            pltpu.VMEM((RING, RING, rows, rank), BF16),
            pltpu.SemaphoreType.DMA((RING, RING)),
        ],
        compiler_params=params(24),
    )(place, *held, basis, probes, leaf_blocks)


GROUP = 4


def send_kernel(selector, columns, *outs):
    capacity = outs[0].shape[1]
    blocks = selector.shape[1]
    for s in range(outs[0].shape[0]):
        moved = jnp.dot(
            selector[...], columns[:, s].reshape(blocks, BLK), preferred_element_type=F32
        ).astype(BF16)
        for i, out in enumerate(outs):
            out[s] = moved[i * capacity : (i + 1) * capacity]


def send(selector, columns, capacity):
    cols, share, near, _ = columns.shape
    count = selector.shape[0] // capacity
    return pl.pallas_call(
        send_kernel,
        grid=(share // GROUP,),
        out_shape=[jax.ShapeDtypeStruct((share, capacity, BLK), BF16)] * count,
        in_specs=[
            pl.BlockSpec(selector.shape, lambda g: (0, 0)),
            pl.BlockSpec((cols, GROUP, near, BLK), lambda g: (0, g, 0, 0)),
        ],
        out_specs=[pl.BlockSpec((GROUP, capacity, BLK), lambda g: (g, 0, 0))] * count,
        compiler_params=params(24),
    )(selector, columns)


def place_kernel(placer, *refs):
    parts, out = refs[:-1], refs[-1]
    for s in range(out.shape[0]):
        arrived = jnp.concatenate([part[s] for part in parts], axis=0)
        out[s] = jnp.dot(placer[...], arrived, preferred_element_type=F32)


def place_blocks(placer, parts):
    share, capacity, _ = parts[0].shape
    return pl.pallas_call(
        place_kernel,
        grid=(share // GROUP,),
        out_shape=jax.ShapeDtypeStruct((share, placer.shape[0], BLK), F32),
        in_specs=[pl.BlockSpec(placer.shape, lambda g: (0, 0))]
        + [pl.BlockSpec((GROUP, capacity, BLK), lambda g: (g, 0, 0))] * len(parts),
        out_specs=pl.BlockSpec((GROUP, placer.shape[0], BLK), lambda g: (g, 0, 0)),
        compiler_params=params(24),
    )(placer, *parts)


def per_device(omega, u_basis, v_basis, coupling, leaf_blocks, child_map):
    y_me, core, z_me, x_me = (lax.axis_index(a) for a in ALL)
    samples = omega.shape[0]
    local = omega.shape[2]
    rank = u_basis.shape[2]
    rows = 2 * samples
    row_count, col_count = 2 * RING, RING * RING
    near = child_map.size
    owner_rows = near * col_count
    capacity = 2 * owner_rows // row_count
    share = samples // col_count
    a_me = jnp.where(core == 0, x_me, z_me)
    b_me = jnp.where(core == 0, z_me, x_me)

    mine = child_map.reshape(-1)
    mine = jnp.concatenate([mine // owner_rows, mine % owner_rows]).astype(F32)
    both = jnp.concatenate([mine, swap_core(mine)])
    info = jnp.zeros((INFO, rank), F32).at[0, : both.size].set(both)

    v_own = jnp.einsum("scn,cnr->csr", omega, v_basis, preferred_element_type=F32).astype(BF16)
    v_own = v_own.reshape(RING, rows // RING, rank)
    v_got = lax.ppermute(v_own, "core", [(1, 0)])
    u_own = jnp.einsum("scn,cnr->csr", omega, u_basis, preferred_element_type=F32).astype(BF16)
    u_own = u_own.reshape(RING, rows // RING, rank)
    u_got = lax.ppermute(u_own, "core", [(0, 1)])
    pieces = pick(jnp.stack([a_me, core]).astype(jnp.int32), v_own, v_got, u_own, u_got)
    pieces = [pieces[0]] + [ring_zx(pieces[k], True, k) for k in STEPS]
    pieces = sum_split(b_me.astype(jnp.int32).reshape(1), pieces)
    pieces = [pieces[0]] + [ring_zx(pieces[k], False, k) for k in STEPS]
    piece = sum_info(pieces, info)
    weight = lax.dynamic_index_in_dim(coupling, a_me // 2, 0, keepdims=False)
    weight = jnp.where(core == 0, weight.T, weight)
    inner = couple([piece] + [ring_y(piece, k) for k in (1, 2, 3)], weight)
    inner = jnp.stack([inner] + [ring_zx(inner, False, k) for k in (1, 2, 3)])
    held = [inner] + [ring_zx(inner, True, k) for k in (1, 2, 3)]
    swapped = [swap_core(p) for p in held]

    fields = 2 * both.size // 2
    seen = jnp.stack([p[:, rows // 16 : rows // 16 + RING, :fields] for p in held])
    at = jnp.arange(RING)
    z_step, x_step = (z_me - at) % RING, (x_me - at) % RING
    flat = jnp.where(
        core == 0, x_step[None, :] * RING + z_step[:, None], z_step[:, None] * RING + x_step[None, :]
    ).reshape(-1)
    seen = seen.reshape(col_count, RING, 2, 2, near)[flat].astype(jnp.int32)
    seen = seen.transpose(3, 2, 1, 0, 4).reshape(2, row_count, owner_rows)
    dest, home = seen[0], seen[1]
    same = (dest[:, :, None] == dest[:, None, :]).astype(jnp.int32)
    before = (jnp.arange(owner_rows)[None, :] < jnp.arange(owner_rows)[:, None]).astype(jnp.int32)
    order = jnp.sum(same * before[None], axis=2)
    to_step = (dest[0] // 2 - y_me) % RING
    to_other = jnp.where(dest[0] % 2 == core, 0, 1)
    slot = (to_other * RING + to_step) * capacity + order[0]
    selector = (jnp.arange(row_count * capacity)[:, None] == slot[None, :]).astype(BF16)
    arriving = jnp.where(dest == y_me * 2 + core, order, -1)
    spots = jnp.arange(capacity)
    ids = jnp.sum((spots[None, :, None] == arriving[:, None, :]) * (home + 1)[:, None, :], axis=2) - 1
    placer = (jnp.arange(owner_rows)[:, None] == ids.reshape(-1)[None, :]).astype(BF16)

    probes = omega.reshape(samples, 2 * local)

    def columns(samp):
        samp = samp.reshape(2, samples, local // BLK, BLK).transpose(1, 0, 2, 3).reshape(samples, near, BLK)
        got = lax.all_to_all(samp, ("z", "x"), split_axis=0, concat_axis=0, tiled=True)
        return got.reshape(col_count, share, near, BLK)

    def exchange(cols):
        out = send(selector, cols, capacity)
        here, there = out[:RING], [swap_core(p) for p in out[RING:]]
        arrived = [here[0]] + [ring_y(here[k], k) for k in (1, 2, 3)]
        arrived += [there[0]] + [ring_y(there[k], k) for k in (1, 2, 3)]
        return place_blocks(placer, arrived).transpose(1, 0, 2)

    y_place = jnp.stack([x_me, z_me, 1 - core]).astype(jnp.int32)
    z_place = jnp.stack([z_me, x_me, core]).astype(jnp.int32)
    y_cols = columns(expand(y_place, held + swapped, u_basis, probes, leaf_blocks, True))
    z_cols = columns(expand(z_place, held + swapped, v_basis, probes, leaf_blocks, False))
    return exchange(y_cols), exchange(z_cols)


def solution(mesh):
    fine = Mesh(mesh.devices.reshape(RING, 2, RING, RING), ALL)
    return jax.shard_map(
        per_device,
        mesh=fine,
        in_specs=(
            P(None, None, ALL),
            P(None, ALL, None),
            P(None, ALL, None),
            P(),
            P(None, ALL, None, None),
            P(None, ALL),
        ),
        out_specs=(P(("y", "core"), ("z", "x"), None), P(("y", "core"), ("z", "x"), None)),
        check_vma=False,
    )
```

```python
import functools

import jax
import jax.numpy as jnp
from jax import lax
from jax.experimental import pallas as pl
from jax.experimental.pallas import tpu as pltpu
from jax.sharding import Mesh, PartitionSpec as P

BLK = 128
ALL = ("y", "core", "z", "x")
RING = 4
STEPS = (1, 3, 2)
INFO = 8
BF16, F32 = jnp.bfloat16, jnp.float32


def ring_y(x, step):
    return lax.ppermute(x, "y", [(i, (i + step) % RING) for i in range(RING)])


def swap_core(x):
    return lax.ppermute(x, "core", [(0, 1), (1, 0)])


def ring_zx(x, first, step):
    pairs = []
    for core in range(2):
        for zz in range(RING):
            for xx in range(RING):
                along_x = (core == 0) == first
                to_z = zz if along_x else (zz + step) % RING
                to_x = (xx + step) % RING if along_x else xx
                pairs.append(((core * RING + zz) * RING + xx, (core * RING + to_z) * RING + to_x))
    return lax.ppermute(x, ("core", "z", "x"), pairs)


VMEM = pl.BlockSpec(memory_space=pltpu.VMEM)
SMEM = pl.BlockSpec(memory_space=pltpu.SMEM)
HBM = pl.BlockSpec(memory_space=pltpu.HBM)
ANY = pl.BlockSpec(memory_space=pl.ANY)


def cost(flops, moved):
    return pl.CostEstimate(flops=flops, bytes_accessed=moved, transcendentals=0)


def params(mib):
    return pltpu.CompilerParams(vmem_limit_bytes=mib * 2**20)


CORE, OTHER, FIRST, SECOND, KIND = range(5)


def merge_kernel(place, v, u, v_got, u_got, *outs):
    rows = outs[0].shape[0]
    child = place[CORE]
    for k, out in enumerate(outs):
        part = lax.rem(place[FIRST] + k, RING)
        at = pl.ds(pl.multiple_of(lax.rem(part, 2) * rows, rows), rows)

        @pl.when(part < 2)
        def _():
            out[...] = (v[child, at].astype(F32) + v_got[at].astype(F32)).astype(BF16)

        @pl.when(part >= 2)
        def _():
            out[...] = (u[child, at].astype(F32) + u_got[at].astype(F32)).astype(BF16)


def merge(place, v, u, v_got, u_got):
    _, samples, rank = v.shape
    return pl.pallas_call(
        merge_kernel,
        out_shape=[jax.ShapeDtypeStruct((samples // 2, rank), BF16)] * RING,
        in_specs=[SMEM] + [VMEM] * 4,
        out_specs=[VMEM] * RING,
        compiler_params=params(16),
    )(place, v, u, v_got, u_got)


def sum_split_kernel(place, *refs):
    ins, outs = refs[:RING], refs[RING:]
    for k in range(RING):
        at = lax.rem(place[SECOND] + k, RING)
        total = ins[0][at].astype(F32)
        for part in ins[1:]:
            total = total + part[at].astype(F32)
        outs[k][...] = total.astype(BF16)


def sum_split(place, parts):
    parts = [p.reshape(RING, -1, p.shape[-1]) for p in parts]
    return pl.pallas_call(
        sum_split_kernel,
        out_shape=[jax.ShapeDtypeStruct(parts[0].shape[1:], BF16)] * RING,
        in_specs=[SMEM] + [VMEM] * RING,
        out_specs=[VMEM] * RING,
        compiler_params=params(16),
    )(place, *parts)


def sum_info_kernel(a, b, c, d, info, out):
    total = a[...].astype(F32) + b[...].astype(F32) + c[...].astype(F32) + d[...].astype(F32)
    out[...] = jnp.concatenate([total, info[...]], axis=0).astype(BF16)


def sum_info(parts, info):
    rows, rank = parts[0].shape
    return pl.pallas_call(
        sum_info_kernel,
        out_shape=jax.ShapeDtypeStruct((rows + INFO, rank), BF16),
        in_specs=[VMEM] * 5,
        out_specs=VMEM,
        compiler_params=params(16),
    )(*parts, info)


def couple_kernel(place, a, b, c, d, weight, out):
    parts = [r[...].astype(F32) for r in (a, b, c, d)]
    rows = out.shape[0] - INFO
    probe = (parts[0] + parts[1] + parts[2] + parts[3]).astype(BF16)
    infos = [p[rows : rows + 1] for p in parts] + [jnp.zeros((INFO - RING, out.shape[1]), F32)]

    def store(side):
        inner = lax.dot_general(probe, weight[...], (((1,), (side,)), ((), ())), preferred_element_type=F32)
        out[...] = jnp.concatenate([inner[:rows]] + infos, axis=0).astype(BF16)

    @pl.when(place[KIND] == 0)
    def _():
        store(1)

    @pl.when(place[KIND] == 1)
    def _():
        store(0)


def couple(place, parts, weight):
    return pl.pallas_call(
        couple_kernel,
        out_shape=jax.ShapeDtypeStruct(parts[0].shape, BF16),
        in_specs=[SMEM] + [VMEM] * 5,
        out_specs=VMEM,
        compiler_params=params(16),
    )(place, *parts, weight)


def expand_kernel(kind, own, place, *refs):
    held, (basis, probes, leaf), rest = refs[:RING], refs[RING : RING + 3], refs[RING + 3 :]
    out, lhs = rest[-2:]
    if own and kind == 0:
        out, seen, lhs = rest[-3:]
        for j in range(RING):
            for m in range(RING):
                seen[j, m] = held[j][m, -2 * INFO :, :BLK]
    child = place[CORE if own else OTHER]
    a_me, b_me = (place[FIRST], place[SECOND]) if own else (place[SECOND], place[FIRST])
    for j in range(RING):
        a = lax.rem(a_me + RING - j, RING)

        @pl.when(a // 2 == kind)
        def _():
            for m in range(RING):
                lhs[lax.rem(a, 2), lax.rem(b_me + RING - m, RING)] = held[j][m]

    rows = lhs.shape[2] - INFO
    rank = lhs.shape[3]
    _, count, size, _ = leaf.shape
    done = []
    for t in range(count):
        at = slice(t * size, (t + 1) * size)
        low = lax.dot_general(
            lhs[...].reshape(-1, rank), basis[at], (((1,), (1,)), ((), ())), preferred_element_type=F32
        )
        low = jnp.concatenate([low[i : i + rows] for i in range(0, low.shape[0], rows + INFO)], axis=0)
        near = lax.dot_general(
            probes[child, :, at], leaf[child, t], (((1,), (1 - kind,)), ((), ())), preferred_element_type=F32
        )
        done.append(low + near)
    done = jnp.concatenate(done, axis=1).reshape(done[0].shape[0], -1, BLK)
    if not own:
        done = jnp.concatenate([rest[0][...].astype(F32), done], axis=1)
    out[...] = done.astype(BF16)


def expand(kind, place, held, basis, probes, leaf_blocks, before=None):
    local, rank = basis.shape
    samples = probes.shape[1]
    own = before is None
    blocks = local // BLK * (1 if own else 2)
    rest = [] if own else [before]
    shapes = [jax.ShapeDtypeStruct((samples, blocks, BLK), BF16)]
    if own and kind == 0:
        shapes.append(jax.ShapeDtypeStruct((RING, RING, 2 * INFO, BLK), BF16))
    got = pl.pallas_call(
        functools.partial(expand_kernel, kind, own),
        in_specs=[SMEM] + [VMEM] * (RING + 3 + len(rest)),
        out_specs=[VMEM] * len(shapes),
        scratch_shapes=[pltpu.VMEM((2, RING) + held[0].shape[1:], BF16)],
        out_shape=shapes,
        compiler_params=params(24),
        cost_estimate=cost(2 * samples * local * (rank + 256), 6 * 2**20),
    )(place, *held, basis, probes, leaf_blocks, *rest)
    return got if len(got) > 1 else got[0]


GROUP = 10


def send_kernel(selector, columns, *outs):
    _, share, capacity, _ = outs[0].shape
    blocks = selector.shape[1]
    for s in range(0, share, 2):
        pair = jnp.concatenate([columns[:, s + i].reshape(blocks, BLK) for i in range(2)], axis=1)
        moved = jnp.dot(selector[...], pair, preferred_element_type=F32).astype(BF16)
        for i in range(2 * RING):
            for h in range(2):
                outs[i % RING][i // RING, s + h] = moved[
                    i * capacity : (i + 1) * capacity, h * BLK : (h + 1) * BLK
                ]


def send(selector, columns, capacity):
    cols, share, near, _ = columns.shape
    return pl.pallas_call(
        send_kernel,
        grid=(share // GROUP,),
        out_shape=[jax.ShapeDtypeStruct((2, share, capacity, BLK), BF16)] * RING,
        in_specs=[
            pl.BlockSpec(selector.shape, lambda g: (0, 0)),
            pl.BlockSpec((cols, GROUP, near, BLK), lambda g: (0, g, 0, 0)),
        ],
        out_specs=[pl.BlockSpec((2, GROUP, capacity, BLK), lambda g: (0, g, 0, 0))] * RING,
        compiler_params=params(32),
        cost_estimate=cost(2 * selector.size * share * BLK, 8 * 2**20),
    )(selector, columns)


def place_kernel(placer, *refs):
    parts, out = refs[:-1], refs[-1]
    for s in range(0, out.shape[0], 2):
        arrived = jnp.concatenate(
            [jnp.concatenate([part[0, s], part[0, s + 1]], axis=1) for part in parts], axis=0
        )
        got = jnp.dot(placer[...], arrived, preferred_element_type=F32)
        out[s] = got[:, :BLK]
        out[s + 1] = got[:, BLK:]


def place_blocks(placer, near):
    far = [swap_core(p) for p in near]
    _, share, capacity, _ = near[0].shape
    spec = lambda half: pl.BlockSpec((1, GROUP, capacity, BLK), lambda g: (half, g, 0, 0))
    return pl.pallas_call(
        place_kernel,
        grid=(share // GROUP,),
        out_shape=jax.ShapeDtypeStruct((share, placer.shape[0], BLK), F32),
        in_specs=[pl.BlockSpec(placer.shape, lambda g: (0, 0))] + [spec(0)] * RING + [spec(1)] * RING,
        out_specs=pl.BlockSpec((GROUP, placer.shape[0], BLK), lambda g: (g, 0, 0)),
        compiler_params=params(32),
        cost_estimate=cost(2 * placer.size * share * BLK, 10 * 2**20),
    )(placer, *near, *far).transpose(1, 0, 2)


def whole(*values):
    return jnp.stack(values).astype(jnp.int32)


def per_device(omega, u_basis, v_basis, coupling, leaf_blocks, child_map):
    y_me, core, z_me, x_me = (lax.axis_index(a) for a in ALL)
    samples = omega.shape[0]
    rank = u_basis.shape[2]
    rows = 2 * samples
    row_count, col_count = 2 * RING, RING * RING
    near = child_map.size
    owner_rows = near * col_count
    capacity = 2 * owner_rows // row_count
    share = samples // col_count
    a_me = jnp.where(core == 0, x_me, z_me)
    b_me = jnp.where(core == 0, z_me, x_me)

    mine = jnp.where(core == 0, child_map, child_map[::-1]).reshape(-1)
    mine = jnp.concatenate([mine // owner_rows, mine % owner_rows]).astype(F32)
    both = jnp.concatenate([mine, swap_core(mine)])
    info = jnp.zeros((INFO, rank), F32).at[0, : both.size].set(both)

    spot = whole(core, 1 - core, a_me, b_me, a_me // 2)
    probes = omega.transpose(1, 0, 2)
    own, got = [], []
    for basis in (v_basis, u_basis):
        own.append(jnp.einsum("scn,cnr->csr", omega, basis, preferred_element_type=F32).astype(BF16))
        got.append(swap_core(lax.dynamic_index_in_dim(own[-1], 1 - core, 0, keepdims=False)))
    pieces = merge(spot, *own, *got)
    coupling, u_late, pieces = lax.optimization_barrier((coupling, u_basis, pieces))
    weight = lax.dynamic_index_in_dim(coupling, core, 0, keepdims=False)
    u_parts = [lax.dynamic_index_in_dim(u_late, c, 0, keepdims=False) for c in (core, 1 - core)]
    pieces = [pieces[0]] + [ring_zx(pieces[k], True, k) for k in STEPS]
    pieces = sum_split(spot, pieces)
    pieces = [pieces[0]] + [ring_zx(pieces[k], False, k) for k in STEPS]
    piece = sum_info(pieces, info)
    inner = couple(spot, [piece] + [ring_y(piece, k) for k in (1, 2, 3)], weight)
    inner = jnp.stack([inner] + [ring_zx(inner, False, k) for k in (1, 2, 3)])
    u_parts, probes, inner = lax.optimization_barrier((u_parts, probes, inner))
    held = [inner] + [ring_zx(inner, True, k) for k in (1, 2, 3)]
    swapped = [swap_core(p) for p in held]

    first, seen = expand(0, spot, held, u_parts[0], probes, leaf_blocks)
    y_samp = expand(0, spot, swapped, u_parts[1], probes, leaf_blocks, first)
    seen, y_samp, v_late = lax.optimization_barrier((seen, y_samp, v_basis))
    v_parts = [lax.dynamic_index_in_dim(v_late, c, 0, keepdims=False) for c in (core, 1 - core)]
    first = expand(1, spot, held, v_parts[0], probes, leaf_blocks)
    z_samp = expand(1, spot, swapped, v_parts[1], probes, leaf_blocks, first)

    fields = both.size
    seen = seen[:, :, INFO : INFO + RING, :fields]
    at = jnp.arange(RING)
    z_step, x_step = (z_me - at) % RING, (x_me - at) % RING
    flat = jnp.where(
        core == 0, x_step[None, :] * RING + z_step[:, None], z_step[:, None] * RING + x_step[None, :]
    ).reshape(-1)
    seen = seen.reshape(col_count, RING, 2, 2, near)[flat].astype(jnp.int32)
    seen = seen.transpose(3, 2, 1, 0, 4).reshape(2, row_count, owner_rows)
    dest, home = seen[0], seen[1]
    same = (dest[:, :, None] == dest[:, None, :]).astype(jnp.int32)
    before = (jnp.arange(owner_rows)[None, :] < jnp.arange(owner_rows)[:, None]).astype(jnp.int32)
    order = jnp.sum(same * before[None], axis=2)

    step = (dest[0] // 2 - y_me) % RING
    slot = (jnp.where(dest[0] % 2 == core, 0, RING) + step) * capacity + order[0]
    selector = (jnp.arange(row_count * capacity)[:, None] == slot[None, :]).astype(BF16)
    arriving = jnp.where(dest == y_me * 2 + core, order, -1)
    spots = jnp.arange(capacity)
    ids = jnp.sum((spots[None, :, None] == arriving[:, None, :]) * (home + 1)[:, None, :], axis=2) - 1
    placer = (jnp.arange(owner_rows)[:, None] == ids.reshape(-1)[None, :]).astype(BF16)

    def columns(samp):
        got = lax.all_to_all(samp, ("z", "x"), split_axis=0, concat_axis=0, tiled=True)
        return got.reshape(col_count, share, near, BLK)

    y_cols = columns(y_samp)
    z_samp, y_cols = lax.optimization_barrier((z_samp, y_cols))
    y_out = send(selector, y_cols, capacity)
    y_out = [y_out[0]] + [ring_y(y_out[k], k) for k in (1, 2, 3)]
    z_out = list(send(selector, columns(z_samp), capacity))
    parent_y = place_blocks(placer, y_out)
    z_out[2], parent_y = lax.optimization_barrier((z_out[2], parent_y))
    z_out = [z_out[0]] + [ring_y(z_out[k], k) for k in (1, 2, 3)]
    return parent_y, place_blocks(placer, z_out)


def solution(mesh):
    fine = Mesh(mesh.devices.reshape(RING, 2, RING, RING), ALL)
    return jax.shard_map(
        per_device,
        mesh=fine,
        in_specs=(
            P(None, None, ALL),
            P(None, ALL, None),
            P(None, ALL, None),
            P(),
            P(None, ALL, None, None),
            P(None, ALL),
        ),
        out_specs=(P(("y", "core"), ("z", "x"), None), P(("y", "core"), ("z", "x"), None)),
        check_vma=False,
    )
```

```python
import functools

import jax
import jax.numpy as jnp
from jax import lax
from jax.experimental import pallas as pl
from jax.experimental.pallas import tpu as pltpu
from jax.sharding import Mesh, PartitionSpec as P

BLK = 128
ALL = ("y", "core", "z", "x")
RING = 4
STEPS = (1, 3, 2)
INFO = 8
BF16, F32 = jnp.bfloat16, jnp.float32


def ring_y(x, step):
    return lax.ppermute(x, "y", [(i, (i + step) % RING) for i in range(RING)])


def swap_core(x):
    return lax.ppermute(x, "core", [(0, 1), (1, 0)])


def ring_zx(x, first, step):
    pairs = []
    for core in range(2):
        for zz in range(RING):
            for xx in range(RING):
                along_x = (core == 0) == first
                to_z = zz if along_x else (zz + step) % RING
                to_x = (xx + step) % RING if along_x else xx
                pairs.append(((core * RING + zz) * RING + xx, (core * RING + to_z) * RING + to_x))
    return lax.ppermute(x, ("core", "z", "x"), pairs)


VMEM = pl.BlockSpec(memory_space=pltpu.VMEM)
SMEM = pl.BlockSpec(memory_space=pltpu.SMEM)
HBM = pl.BlockSpec(memory_space=pltpu.HBM)
ANY = pl.BlockSpec(memory_space=pl.ANY)


def cost(flops, moved):
    return pl.CostEstimate(flops=flops, bytes_accessed=moved, transcendentals=0)


def params(mib):
    return pltpu.CompilerParams(vmem_limit_bytes=mib * 2**20)


CORE, OTHER, FIRST, SECOND, KIND = range(5)


def merge_kernel(place, v, u, v_got, u_got, *outs):
    rows = outs[0].shape[0]
    for k, out in enumerate(outs):
        part = lax.rem(place[FIRST] + k, RING)
        at = pl.ds(pl.multiple_of(lax.rem(part, 2) * rows, rows), rows)

        @pl.when(part < 2)
        def _():
            out[...] = (v[at].astype(F32) + v_got[at].astype(F32)).astype(BF16)

        @pl.when(part >= 2)
        def _():
            out[...] = (u[at].astype(F32) + u_got[at].astype(F32)).astype(BF16)


def merge(place, v, u, v_got, u_got):
    samples, rank = v.shape
    return pl.pallas_call(
        merge_kernel,
        out_shape=[jax.ShapeDtypeStruct((samples // 2, rank), BF16)] * RING,
        in_specs=[SMEM] + [VMEM] * 4,
        out_specs=[VMEM] * RING,
        compiler_params=params(16),
    )(place, v, u, v_got, u_got)


def sum_split_kernel(place, *refs):
    ins, outs = refs[:RING], refs[RING:]
    for k in range(RING):
        at = lax.rem(place[SECOND] + k, RING)
        total = ins[0][at].astype(F32)
        for part in ins[1:]:
            total = total + part[at].astype(F32)
        outs[k][...] = total.astype(BF16)


def sum_split(place, parts):
    parts = [p.reshape(RING, -1, p.shape[-1]) for p in parts]
    return pl.pallas_call(
        sum_split_kernel,
        out_shape=[jax.ShapeDtypeStruct(parts[0].shape[1:], BF16)] * RING,
        in_specs=[SMEM] + [VMEM] * RING,
        out_specs=[VMEM] * RING,
        compiler_params=params(16),
    )(place, *parts)


def sum_info_kernel(a, b, c, d, info, out):
    total = a[...].astype(F32) + b[...].astype(F32) + c[...].astype(F32) + d[...].astype(F32)
    out[...] = jnp.concatenate([total, info[...]], axis=0).astype(BF16)


def sum_info(parts, info):
    rows, rank = parts[0].shape
    return pl.pallas_call(
        sum_info_kernel,
        out_shape=jax.ShapeDtypeStruct((rows + INFO, rank), BF16),
        in_specs=[VMEM] * 5,
        out_specs=VMEM,
        compiler_params=params(16),
    )(*parts, info)


def couple_kernel(place, a, b, c, d, weight, out):
    parts = [r[...].astype(F32) for r in (a, b, c, d)]
    rows = out.shape[0] - INFO
    probe = (parts[0] + parts[1] + parts[2] + parts[3]).astype(BF16)
    infos = [p[rows : rows + 1] for p in parts] + [jnp.zeros((INFO - RING, out.shape[1]), F32)]

    def store(side):
        inner = lax.dot_general(probe, weight[...], (((1,), (side,)), ((), ())), preferred_element_type=F32)
        out[...] = jnp.concatenate([inner[:rows]] + infos, axis=0).astype(BF16)

    @pl.when(place[KIND] == 0)
    def _():
        store(1)

    @pl.when(place[KIND] == 1)
    def _():
        store(0)


def couple(place, parts, weight):
    return pl.pallas_call(
        couple_kernel,
        out_shape=jax.ShapeDtypeStruct(parts[0].shape, BF16),
        in_specs=[SMEM] + [VMEM] * 5,
        out_specs=VMEM,
        compiler_params=params(16),
    )(place, *parts, weight)


def expand_kernel(kind, own, place, *refs):
    held, (basis, probes, leaf), rest = refs[:RING], refs[RING : RING + 3], refs[RING + 3 :]
    out, lhs = rest[-2:]
    if own and kind == 0:
        out, seen, lhs = rest[-3:]
        for j in range(RING):
            for m in range(RING):
                seen[j, m] = held[j][m, -2 * INFO :, :BLK]
    child = place[CORE if own else OTHER]
    a_me, b_me = (place[FIRST], place[SECOND]) if own else (place[SECOND], place[FIRST])
    for j in range(RING):
        a = lax.rem(a_me + RING - j, RING)

        @pl.when(a // 2 == kind)
        def _():
            for m in range(RING):
                lhs[lax.rem(a, 2), lax.rem(b_me + RING - m, RING)] = held[j][m]

    rows = lhs.shape[2] - INFO
    rank = lhs.shape[3]
    _, count, size, _ = leaf.shape
    done = []
    for t in range(count):
        at = slice(t * size, (t + 1) * size)
        low = lax.dot_general(
            lhs[...].reshape(-1, rank), basis[at], (((1,), (1,)), ((), ())), preferred_element_type=F32
        )
        low = jnp.concatenate([low[i : i + rows] for i in range(0, low.shape[0], rows + INFO)], axis=0)
        near = lax.dot_general(
            probes[child, :, at], leaf[child, t], (((1,), (1 - kind,)), ((), ())), preferred_element_type=F32
        )
        done.append(low + near)
    done = jnp.concatenate(done, axis=1).reshape(done[0].shape[0], -1, BLK)
    if not own:
        done = jnp.concatenate([rest[0][...].astype(F32), done], axis=1)
    out[...] = done.astype(BF16)


def expand(kind, place, held, basis, probes, leaf_blocks, before=None):
    local, rank = basis.shape
    samples = probes.shape[1]
    own = before is None
    blocks = local // BLK * (1 if own else 2)
    rest = [] if own else [before]
    shapes = [jax.ShapeDtypeStruct((samples, blocks, BLK), BF16)]
    if own and kind == 0:
        shapes.append(jax.ShapeDtypeStruct((RING, RING, 2 * INFO, BLK), BF16))
    got = pl.pallas_call(
        functools.partial(expand_kernel, kind, own),
        in_specs=[SMEM] + [VMEM] * (RING + 3 + len(rest)),
        out_specs=[VMEM] * len(shapes),
        scratch_shapes=[pltpu.VMEM((2, RING) + held[0].shape[1:], BF16)],
        out_shape=shapes,
        compiler_params=params(24),
        cost_estimate=cost(2 * samples * local * (rank + 256), 6 * 2**20),
    )(place, *held, basis, probes, leaf_blocks, *rest)
    return got if len(got) > 1 else got[0]


GROUP = 10


def send_kernel(selector, columns, *outs):
    _, share, capacity, _ = outs[0].shape
    blocks = selector.shape[1]
    for s in range(0, share, 2):
        pair = jnp.concatenate([columns[:, s + i].reshape(blocks, BLK) for i in range(2)], axis=1)
        moved = jnp.dot(selector[...], pair, preferred_element_type=F32).astype(BF16)
        for i in range(2 * RING):
            for h in range(2):
                outs[i % RING][i // RING, s + h] = moved[
                    i * capacity : (i + 1) * capacity, h * BLK : (h + 1) * BLK
                ]


def send(selector, columns, capacity):
    cols, share, near, _ = columns.shape
    return pl.pallas_call(
        send_kernel,
        grid=(share // GROUP,),
        out_shape=[jax.ShapeDtypeStruct((2, share, capacity, BLK), BF16)] * RING,
        in_specs=[
            pl.BlockSpec(selector.shape, lambda g: (0, 0)),
            pl.BlockSpec((cols, GROUP, near, BLK), lambda g: (0, g, 0, 0)),
        ],
        out_specs=[pl.BlockSpec((2, GROUP, capacity, BLK), lambda g: (0, g, 0, 0))] * RING,
        compiler_params=params(32),
        cost_estimate=cost(2 * selector.size * share * BLK, 8 * 2**20),
    )(selector, columns)


def place_kernel(placer, *refs):
    parts, out = refs[:-1], refs[-1]
    for s in range(0, out.shape[0], 2):
        arrived = jnp.concatenate(
            [jnp.concatenate([part[0, s], part[0, s + 1]], axis=1) for part in parts], axis=0
        )
        got = jnp.dot(placer[...], arrived, preferred_element_type=F32)
        out[s] = got[:, :BLK]
        out[s + 1] = got[:, BLK:]


def place_blocks(placer, near, far_first):
    far = [far_first] + [swap_core(p) for p in near[1:]]
    _, share, capacity, _ = near[0].shape
    spec = lambda half: pl.BlockSpec((1, GROUP, capacity, BLK), lambda g: (half, g, 0, 0))
    return pl.pallas_call(
        place_kernel,
        grid=(share // GROUP,),
        out_shape=jax.ShapeDtypeStruct((share, placer.shape[0], BLK), F32),
        in_specs=[pl.BlockSpec(placer.shape, lambda g: (0, 0))] + [spec(0)] * RING + [spec(1)] * RING,
        out_specs=pl.BlockSpec((GROUP, placer.shape[0], BLK), lambda g: (g, 0, 0)),
        compiler_params=params(32),
        cost_estimate=cost(2 * placer.size * share * BLK, 10 * 2**20),
    )(placer, *near, *far).transpose(1, 0, 2)


def whole(*values):
    return jnp.stack(values).astype(jnp.int32)


def per_device(omega, u_basis, v_basis, coupling, leaf_blocks, child_map):
    y_me, core, z_me, x_me = (lax.axis_index(a) for a in ALL)
    samples = omega.shape[0]
    rank = u_basis.shape[2]
    rows = 2 * samples
    row_count, col_count = 2 * RING, RING * RING
    near = child_map.size
    owner_rows = near * col_count
    capacity = 2 * owner_rows // row_count
    share = samples // col_count
    a_me = jnp.where(core == 0, x_me, z_me)
    b_me = jnp.where(core == 0, z_me, x_me)

    mine = jnp.where(core == 0, child_map, child_map[::-1]).reshape(-1)
    mine = jnp.concatenate([mine // owner_rows, mine % owner_rows]).astype(F32)
    both = jnp.concatenate([mine, swap_core(mine)])
    info = jnp.zeros((INFO, rank), F32).at[0, : both.size].set(both)

    spot = whole(core, 1 - core, a_me, b_me, a_me // 2)
    probes = omega.transpose(1, 0, 2)
    own, got = [], []
    for basis in (v_basis, u_basis):
        both_parts = jnp.einsum("scn,cnr->csr", omega, basis, preferred_element_type=F32).astype(BF16)
        own.append(lax.dynamic_index_in_dim(both_parts, core, 0, keepdims=False))
        got.append(swap_core(lax.dynamic_index_in_dim(both_parts, 1 - core, 0, keepdims=False)))
    pieces = merge(spot, *own, *got)
    coupling, u_late, pieces = lax.optimization_barrier((coupling, u_basis, pieces))
    weight = lax.dynamic_index_in_dim(coupling, core, 0, keepdims=False)
    u_own = lax.dynamic_index_in_dim(u_late, core, 0, keepdims=False)
    pieces = [pieces[0]] + [ring_zx(pieces[k], True, k) for k in STEPS]
    pieces = sum_split(spot, pieces)
    pieces = [pieces[0]] + [ring_zx(pieces[k], False, k) for k in STEPS]
    piece = sum_info(pieces, info)
    u_own, probes, piece, u_late = lax.optimization_barrier((u_own, probes, piece, u_late))
    u_other = lax.dynamic_index_in_dim(u_late, 1 - core, 0, keepdims=False)
    inner = couple(spot, [piece] + [ring_y(piece, k) for k in (1, 2, 3)], weight)
    inner = jnp.stack([inner] + [ring_zx(inner, False, k) for k in (1, 2, 3)])
    u_other, inner = lax.optimization_barrier((u_other, inner))
    held = [inner] + [ring_zx(inner, True, k) for k in (1, 2, 3)]
    swapped = [swap_core(p) for p in held]

    first, seen = expand(0, spot, held, u_own, probes, leaf_blocks)
    y_samp = expand(0, spot, swapped, u_other, probes, leaf_blocks, first)
    seen, y_samp, v_late, count = lax.optimization_barrier((seen, y_samp, v_basis, jnp.arange(owner_rows)))
    v_parts = [lax.dynamic_index_in_dim(v_late, c, 0, keepdims=False) for c in (core, 1 - core)]
    first = expand(1, spot, held, v_parts[0], probes, leaf_blocks)
    z_samp = expand(1, spot, swapped, v_parts[1], probes, leaf_blocks, first)

    fields = both.size
    seen = seen[:, :, INFO : INFO + RING, :fields]
    at = jnp.arange(RING)
    z_step, x_step = (z_me - at) % RING, (x_me - at) % RING
    flat = jnp.where(
        core == 0, x_step[None, :] * RING + z_step[:, None], z_step[:, None] * RING + x_step[None, :]
    ).reshape(-1)
    seen = seen.reshape(col_count, RING, 2, 2, near)[flat].astype(jnp.int32)
    seen = seen.transpose(3, 2, 1, 0, 4).reshape(2, row_count, owner_rows)
    dest, home = seen[0], seen[1]
    same = (dest[:, :, None] == dest[:, None, :]).astype(jnp.int32)
    before = (count[None, :] < count[:, None]).astype(jnp.int32)
    order = jnp.sum(same * before[None], axis=2)

    step = (dest[0] // 2 - y_me) % RING
    slot = (jnp.where(dest[0] % 2 == core, 0, RING) + step) * capacity + order[0]
    selector = (jnp.arange(row_count * capacity)[:, None] == slot[None, :]).astype(BF16)
    arriving = jnp.where(dest == y_me * 2 + core, order, -1)
    spots = jnp.arange(capacity)
    ids = jnp.sum((spots[None, :, None] == arriving[:, None, :]) * (home + 1)[:, None, :], axis=2) - 1
    placer = (jnp.arange(owner_rows)[:, None] == ids.reshape(-1)[None, :]).astype(BF16)

    def columns(samp):
        got = lax.all_to_all(samp, ("z", "x"), split_axis=0, concat_axis=0, tiled=True)
        return got.reshape(col_count, share, near, BLK)

    y_cols = columns(y_samp)
    z_samp, y_cols = lax.optimization_barrier((z_samp, y_cols))
    y_out = send(selector, y_cols, capacity)
    y_out = [y_out[0]] + [ring_y(y_out[k], k) for k in (1, 2, 3)]
    z_out = list(send(selector, columns(z_samp), capacity))
    z_far = swap_core(z_out[0])
    y_out[1:], z_far = lax.optimization_barrier((y_out[1:], z_far))
    parent_y = place_blocks(placer, y_out, swap_core(y_out[0]))
    z_out[2], parent_y = lax.optimization_barrier((z_out[2], parent_y))
    z_out = [z_out[0]] + [ring_y(z_out[k], k) for k in (1, 2, 3)]
    return parent_y, place_blocks(placer, z_out, z_far)


def solution(mesh):
    fine = Mesh(mesh.devices.reshape(RING, 2, RING, RING), ALL)
    return jax.shard_map(
        per_device,
        mesh=fine,
        in_specs=(
            P(None, None, ALL),
            P(None, ALL, None),
            P(None, ALL, None),
            P(),
            P(None, ALL, None, None),
            P(None, ALL),
        ),
        out_specs=(P(("y", "core"), ("z", "x"), None), P(("y", "core"), ("z", "x"), None)),
        check_vma=False,
    )
```

```python
import functools

import jax
import jax.numpy as jnp
from jax import lax
from jax.experimental import pallas as pl
from jax.experimental.pallas import tpu as pltpu
from jax.sharding import Mesh, PartitionSpec as P

BLK = 128
ALL = ("y", "core", "z", "x")
RING = 4
STEPS = (1, 3, 2)
INFO = 8
BF16, F32 = jnp.bfloat16, jnp.float32


def ring_y(x, step):
    return lax.ppermute(x, "y", [(i, (i + step) % RING) for i in range(RING)])


def swap_core(x):
    return lax.ppermute(x, "core", [(0, 1), (1, 0)])


def ring_zx(x, first, step):
    pairs = []
    for core in range(2):
        for zz in range(RING):
            for xx in range(RING):
                along_x = (core == 0) == first
                to_z = zz if along_x else (zz + step) % RING
                to_x = (xx + step) % RING if along_x else xx
                pairs.append(((core * RING + zz) * RING + xx, (core * RING + to_z) * RING + to_x))
    return lax.ppermute(x, ("core", "z", "x"), pairs)


VMEM = pl.BlockSpec(memory_space=pltpu.VMEM)
SMEM = pl.BlockSpec(memory_space=pltpu.SMEM)
HBM = pl.BlockSpec(memory_space=pltpu.HBM)
ANY = pl.BlockSpec(memory_space=pl.ANY)


def cost(flops, moved):
    return pl.CostEstimate(flops=flops, bytes_accessed=moved, transcendentals=0)


def params(mib):
    return pltpu.CompilerParams(vmem_limit_bytes=mib * 2**20)


CORE, OTHER, FIRST, SECOND, KIND = range(5)


def merge_kernel(place, v, u, v_got, u_got, *outs):
    rows = outs[0].shape[0]
    for k, out in enumerate(outs):
        part = lax.rem(place[FIRST] + k, RING)
        at = pl.ds(pl.multiple_of(lax.rem(part, 2) * rows, rows), rows)

        @pl.when(part < 2)
        def _():
            out[...] = (v[at].astype(F32) + v_got[at].astype(F32)).astype(BF16)

        @pl.when(part >= 2)
        def _():
            out[...] = (u[at].astype(F32) + u_got[at].astype(F32)).astype(BF16)


def merge(place, v, u, v_got, u_got):
    samples, rank = v.shape
    return pl.pallas_call(
        merge_kernel,
        out_shape=[jax.ShapeDtypeStruct((samples // 2, rank), BF16)] * RING,
        in_specs=[SMEM] + [VMEM] * 4,
        out_specs=[VMEM] * RING,
        compiler_params=params(16),
    )(place, v, u, v_got, u_got)


def sum_split_kernel(place, *refs):
    ins, outs = refs[:RING], refs[RING:]
    for k in range(RING):
        at = lax.rem(place[SECOND] + k, RING)
        total = ins[0][at].astype(F32)
        for part in ins[1:]:
            total = total + part[at].astype(F32)
        outs[k][...] = total.astype(BF16)


def sum_split(place, parts):
    parts = [p.reshape(RING, -1, p.shape[-1]) for p in parts]
    return pl.pallas_call(
        sum_split_kernel,
        out_shape=[jax.ShapeDtypeStruct(parts[0].shape[1:], BF16)] * RING,
        in_specs=[SMEM] + [VMEM] * RING,
        out_specs=[VMEM] * RING,
        compiler_params=params(16),
    )(place, *parts)


def sum_info_kernel(a, b, c, d, info, out):
    total = a[...].astype(F32) + b[...].astype(F32) + c[...].astype(F32) + d[...].astype(F32)
    out[...] = jnp.concatenate([total, info[...]], axis=0).astype(BF16)


def sum_info(parts, info):
    rows, rank = parts[0].shape
    return pl.pallas_call(
        sum_info_kernel,
        out_shape=jax.ShapeDtypeStruct((rows + INFO, rank), BF16),
        in_specs=[VMEM] * 5,
        out_specs=VMEM,
        compiler_params=params(16),
    )(*parts, info)


def couple_kernel(place, a, b, c, d, weight, out):
    parts = [r[...].astype(F32) for r in (a, b, c, d)]
    rows = out.shape[0] - INFO
    probe = (parts[0] + parts[1] + parts[2] + parts[3]).astype(BF16)
    infos = [p[rows : rows + 1] for p in parts] + [jnp.zeros((INFO - RING, out.shape[1]), F32)]

    def store(side):
        inner = lax.dot_general(probe, weight[...], (((1,), (side,)), ((), ())), preferred_element_type=F32)
        out[...] = jnp.concatenate([inner[:rows]] + infos, axis=0).astype(BF16)

    @pl.when(place[KIND] == 0)
    def _():
        store(1)

    @pl.when(place[KIND] == 1)
    def _():
        store(0)


def couple(place, parts, weight):
    return pl.pallas_call(
        couple_kernel,
        out_shape=jax.ShapeDtypeStruct(parts[0].shape, BF16),
        in_specs=[SMEM] + [VMEM] * 5,
        out_specs=VMEM,
        compiler_params=params(16),
    )(place, *parts, weight)


def expand_kernel(kind, own, place, *refs):
    held, (basis, probes, leaf), rest = refs[:RING], refs[RING : RING + 3], refs[RING + 3 :]
    out, lhs = rest[-2:]
    if own and kind == 0:
        out, seen, lhs = rest[-3:]
        for j in range(RING):
            for m in range(RING):
                seen[j, m] = held[j][m, -2 * INFO :, :BLK]
    child = place[CORE if own else OTHER]
    a_me, b_me = (place[FIRST], place[SECOND]) if own else (place[SECOND], place[FIRST])
    for j in range(RING):
        a = lax.rem(a_me + RING - j, RING)

        @pl.when(a // 2 == kind)
        def _():
            for m in range(RING):
                lhs[lax.rem(a, 2), lax.rem(b_me + RING - m, RING)] = held[j][m]

    rows = lhs.shape[2] - INFO
    rank = lhs.shape[3]
    _, count, size, _ = leaf.shape
    done = []
    for t in range(count):
        at = slice(t * size, (t + 1) * size)
        low = lax.dot_general(
            lhs[...].reshape(-1, rank), basis[at], (((1,), (1,)), ((), ())), preferred_element_type=F32
        )
        low = jnp.concatenate([low[i : i + rows] for i in range(0, low.shape[0], rows + INFO)], axis=0)
        near = lax.dot_general(
            probes[child, :, at], leaf[child, t], (((1,), (1 - kind,)), ((), ())), preferred_element_type=F32
        )
        done.append(low + near)
    done = jnp.concatenate(done, axis=1).reshape(done[0].shape[0], -1, BLK)
    if not own:
        done = jnp.concatenate([rest[0][...].astype(F32), done], axis=1)
    out[...] = done.astype(BF16)


def expand(kind, place, held, basis, probes, leaf_blocks, before=None):
    local, rank = basis.shape
    samples = probes.shape[1]
    own = before is None
    blocks = local // BLK * (1 if own else 2)
    rest = [] if own else [before]
    shapes = [jax.ShapeDtypeStruct((samples, blocks, BLK), BF16)]
    if own and kind == 0:
        shapes.append(jax.ShapeDtypeStruct((RING, RING, 2 * INFO, BLK), BF16))
    got = pl.pallas_call(
        functools.partial(expand_kernel, kind, own),
        in_specs=[SMEM] + [VMEM] * (RING + 3 + len(rest)),
        out_specs=[VMEM] * len(shapes),
        scratch_shapes=[pltpu.VMEM((2, RING) + held[0].shape[1:], BF16)],
        out_shape=shapes,
        compiler_params=params(24),
        cost_estimate=cost(2 * samples * local * (rank + 256), 6 * 2**20),
    )(place, *held, basis, probes, leaf_blocks, *rest)
    return got if len(got) > 1 else got[0]


GROUP = 10


def send_kernel(selector, columns, *outs):
    _, share, capacity, _ = outs[0].shape
    blocks = selector.shape[1]
    for s in range(0, share, 2):
        pair = jnp.concatenate([columns[:, s + i].reshape(blocks, BLK) for i in range(2)], axis=1)
        moved = jnp.dot(selector[...], pair, preferred_element_type=F32).astype(BF16)
        for i in range(2 * RING):
            for h in range(2):
                outs[i % RING][i // RING, s + h] = moved[
                    i * capacity : (i + 1) * capacity, h * BLK : (h + 1) * BLK
                ]


def send(selector, columns, capacity):
    cols, share, near, _ = columns.shape
    return pl.pallas_call(
        send_kernel,
        grid=(share // GROUP,),
        out_shape=[jax.ShapeDtypeStruct((2, share, capacity, BLK), BF16)] * RING,
        in_specs=[
            pl.BlockSpec(selector.shape, lambda g: (0, 0)),
            pl.BlockSpec((cols, GROUP, near, BLK), lambda g: (0, g, 0, 0)),
        ],
        out_specs=[pl.BlockSpec((2, GROUP, capacity, BLK), lambda g: (0, g, 0, 0))] * RING,
        compiler_params=params(32),
        cost_estimate=cost(2 * selector.size * share * BLK, 8 * 2**20),
    )(selector, columns)


def place_kernel(placer, *refs):
    parts, out = refs[:-1], refs[-1]
    for s in range(0, out.shape[0], 2):
        arrived = jnp.concatenate(
            [jnp.concatenate([part[0, s], part[0, s + 1]], axis=1) for part in parts], axis=0
        )
        got = jnp.dot(placer[...], arrived, preferred_element_type=F32)
        out[s] = got[:, :BLK]
        out[s + 1] = got[:, BLK:]


def place_blocks(placer, near):
    far = [swap_core(p) for p in near]
    _, share, capacity, _ = near[0].shape
    spec = lambda half: pl.BlockSpec((1, GROUP, capacity, BLK), lambda g: (half, g, 0, 0))
    return pl.pallas_call(
        place_kernel,
        grid=(share // GROUP,),
        out_shape=jax.ShapeDtypeStruct((share, placer.shape[0], BLK), F32),
        in_specs=[pl.BlockSpec(placer.shape, lambda g: (0, 0))] + [spec(0)] * RING + [spec(1)] * RING,
        out_specs=pl.BlockSpec((GROUP, placer.shape[0], BLK), lambda g: (g, 0, 0)),
        compiler_params=params(32),
        cost_estimate=cost(2 * placer.size * share * BLK, 10 * 2**20),
    )(placer, *near, *far).transpose(1, 0, 2)


def whole(*values):
    return jnp.stack(values).astype(jnp.int32)


def per_device(omega, u_basis, v_basis, coupling, leaf_blocks, child_map):
    y_me, core, z_me, x_me = (lax.axis_index(a) for a in ALL)
    samples = omega.shape[0]
    rank = u_basis.shape[2]
    rows = 2 * samples
    row_count, col_count = 2 * RING, RING * RING
    near = child_map.size
    owner_rows = near * col_count
    capacity = 2 * owner_rows // row_count
    share = samples // col_count
    a_me = jnp.where(core == 0, x_me, z_me)
    b_me = jnp.where(core == 0, z_me, x_me)

    mine = jnp.where(core == 0, child_map, child_map[::-1]).reshape(-1)
    mine = jnp.concatenate([mine // owner_rows, mine % owner_rows]).astype(F32)
    both = jnp.concatenate([mine, swap_core(mine)])
    info = jnp.zeros((INFO, rank), F32).at[0, : both.size].set(both)

    spot = whole(core, 1 - core, a_me, b_me, a_me // 2)
    probes = omega.transpose(1, 0, 2)
    own, got = [], []
    for basis in (v_basis, u_basis):
        both_parts = jnp.einsum("scn,cnr->csr", omega, basis, preferred_element_type=F32).astype(BF16)
        own.append(lax.dynamic_index_in_dim(both_parts, core, 0, keepdims=False))
        got.append(swap_core(lax.dynamic_index_in_dim(both_parts, 1 - core, 0, keepdims=False)))
    pieces = merge(spot, *own, *got)
    coupling, u_late, pieces = lax.optimization_barrier((coupling, u_basis, pieces))
    weight = lax.dynamic_index_in_dim(coupling, core, 0, keepdims=False)
    u_own = lax.dynamic_index_in_dim(u_late, core, 0, keepdims=False)
    pieces = [pieces[0]] + [ring_zx(pieces[k], True, k) for k in STEPS]
    pieces = sum_split(spot, pieces)
    pieces = [pieces[0]] + [ring_zx(pieces[k], False, k) for k in STEPS]
    piece = sum_info(pieces, info)
    u_own, probes, piece, u_late = lax.optimization_barrier((u_own, probes, piece, u_late))
    u_other = lax.dynamic_index_in_dim(u_late, 1 - core, 0, keepdims=False)
    inner = couple(spot, [piece] + [ring_y(piece, k) for k in (1, 2, 3)], weight)
    inner = jnp.stack([inner] + [ring_zx(inner, False, k) for k in (1, 2, 3)])
    u_other, inner = lax.optimization_barrier((u_other, inner))
    held = [inner] + [ring_zx(inner, True, k) for k in (1, 2, 3)]
    swapped = [swap_core(p) for p in held]

    first, seen = expand(0, spot, held, u_own, probes, leaf_blocks)
    y_samp = expand(0, spot, swapped, u_other, probes, leaf_blocks, first)
    seen, y_samp, v_late, count = lax.optimization_barrier((seen, y_samp, v_basis, jnp.arange(owner_rows)))
    v_parts = [lax.dynamic_index_in_dim(v_late, c, 0, keepdims=False) for c in (core, 1 - core)]
    first = expand(1, spot, held, v_parts[0], probes, leaf_blocks)
    z_samp = expand(1, spot, swapped, v_parts[1], probes, leaf_blocks, first)

    fields = both.size
    seen = seen[:, :, INFO : INFO + RING, :fields]
    at = jnp.arange(RING)
    z_step, x_step = (z_me - at) % RING, (x_me - at) % RING
    flat = jnp.where(
        core == 0, x_step[None, :] * RING + z_step[:, None], z_step[:, None] * RING + x_step[None, :]
    ).reshape(-1)
    seen = seen.reshape(col_count, RING, 2, 2, near)[flat].astype(jnp.int32)
    seen = seen.transpose(3, 2, 1, 0, 4).reshape(2, row_count, owner_rows)
    dest, home = seen[0], seen[1]
    same = (dest[:, :, None] == dest[:, None, :]).astype(jnp.int32)
    before = (count[None, :] < count[:, None]).astype(jnp.int32)
    order = jnp.sum(same * before[None], axis=2)

    step = (dest[0] // 2 - y_me) % RING
    slot = (jnp.where(dest[0] % 2 == core, 0, RING) + step) * capacity + order[0]
    selector = (jnp.arange(row_count * capacity)[:, None] == slot[None, :]).astype(BF16)
    arriving = jnp.where(dest == y_me * 2 + core, order, -1)
    spots = jnp.arange(capacity)
    ids = jnp.sum((spots[None, :, None] == arriving[:, None, :]) * (home + 1)[:, None, :], axis=2) - 1
    placer = (jnp.arange(owner_rows)[:, None] == ids.reshape(-1)[None, :]).astype(BF16)

    def columns(samp):
        got = lax.all_to_all(samp, ("z", "x"), split_axis=0, concat_axis=0, tiled=True)
        return got.reshape(col_count, share, near, BLK)

    y_cols = columns(y_samp)
    z_samp, y_cols = lax.optimization_barrier((z_samp, y_cols))
    y_out = send(selector, y_cols, capacity)
    y_out = [y_out[0]] + [ring_y(y_out[k], k) for k in (1, 2, 3)]
    z_out = list(send(selector, columns(z_samp), capacity))
    parent_y = place_blocks(placer, y_out)
    z_out[2], parent_y = lax.optimization_barrier((z_out[2], parent_y))
    z_out = [z_out[0]] + [ring_y(z_out[k], k) for k in (1, 2, 3)]
    return parent_y, place_blocks(placer, z_out)


def solution(mesh):
    fine = Mesh(mesh.devices.reshape(RING, 2, RING, RING), ALL)
    return jax.shard_map(
        per_device,
        mesh=fine,
        in_specs=(
            P(None, None, ALL),
            P(None, ALL, None),
            P(None, ALL, None),
            P(),
            P(None, ALL, None, None),
            P(None, ALL),
        ),
        out_specs=(P(("y", "core"), ("z", "x"), None), P(("y", "core"), ("z", "x"), None)),
        check_vma=False,
    )
```

```python
import functools

import jax
import jax.numpy as jnp
from jax import lax
from jax.experimental import pallas as pl
from jax.experimental.pallas import tpu as pltpu
from jax.sharding import Mesh, PartitionSpec as P

BLK = 128
ALL = ("y", "core", "z", "x")
RING = 4
STEPS = (1, 3, 2)
INFO = 8
BF16, F32 = jnp.bfloat16, jnp.float32


def ring_y(x, step):
    return lax.ppermute(x, "y", [(i, (i + step) % RING) for i in range(RING)])


def swap_core(x):
    return lax.ppermute(x, "core", [(0, 1), (1, 0)])


def ring_zx(x, first, step):
    pairs = []
    for core in range(2):
        for zz in range(RING):
            for xx in range(RING):
                along_x = (core == 0) == first
                to_z = zz if along_x else (zz + step) % RING
                to_x = (xx + step) % RING if along_x else xx
                pairs.append(((core * RING + zz) * RING + xx, (core * RING + to_z) * RING + to_x))
    return lax.ppermute(x, ("core", "z", "x"), pairs)


VMEM = pl.BlockSpec(memory_space=pltpu.VMEM)
SMEM = pl.BlockSpec(memory_space=pltpu.SMEM)
HBM = pl.BlockSpec(memory_space=pltpu.HBM)
ANY = pl.BlockSpec(memory_space=pl.ANY)


def cost(flops, moved):
    return pl.CostEstimate(flops=flops, bytes_accessed=moved, transcendentals=0)


def params(mib):
    return pltpu.CompilerParams(vmem_limit_bytes=mib * 2**20)


CORE, OTHER, FIRST, SECOND, KIND = range(5)


def merge_kernel(place, v, u, v_got, u_got, *outs):
    rows = outs[0].shape[0]
    for k, out in enumerate(outs):
        part = lax.rem(place[FIRST] + k, RING)
        at = pl.ds(pl.multiple_of(lax.rem(part, 2) * rows, rows), rows)

        @pl.when(part < 2)
        def _():
            out[...] = (v[at].astype(F32) + v_got[at].astype(F32)).astype(BF16)

        @pl.when(part >= 2)
        def _():
            out[...] = (u[at].astype(F32) + u_got[at].astype(F32)).astype(BF16)


def merge(place, v, u, v_got, u_got):
    samples, rank = v.shape
    return pl.pallas_call(
        merge_kernel,
        out_shape=[jax.ShapeDtypeStruct((samples // 2, rank), BF16)] * RING,
        in_specs=[SMEM] + [VMEM] * 4,
        out_specs=[VMEM] * RING,
        compiler_params=params(16),
    )(place, v, u, v_got, u_got)


def sum_split_kernel(place, *refs):
    ins, outs = refs[:RING], refs[RING:]
    for k in range(RING):
        at = lax.rem(place[SECOND] + k, RING)
        total = ins[0][at].astype(F32)
        for part in ins[1:]:
            total = total + part[at].astype(F32)
        outs[k][...] = total.astype(BF16)


def sum_split(place, parts):
    parts = [p.reshape(RING, -1, p.shape[-1]) for p in parts]
    return pl.pallas_call(
        sum_split_kernel,
        out_shape=[jax.ShapeDtypeStruct(parts[0].shape[1:], BF16)] * RING,
        in_specs=[SMEM] + [VMEM] * RING,
        out_specs=[VMEM] * RING,
        compiler_params=params(16),
    )(place, *parts)


def sum_info_kernel(a, b, c, d, info, out):
    total = a[...].astype(F32) + b[...].astype(F32) + c[...].astype(F32) + d[...].astype(F32)
    out[...] = jnp.concatenate([total, info[...]], axis=0).astype(BF16)


def sum_info(parts, info):
    rows, rank = parts[0].shape
    return pl.pallas_call(
        sum_info_kernel,
        out_shape=jax.ShapeDtypeStruct((rows + INFO, rank), BF16),
        in_specs=[VMEM] * 5,
        out_specs=VMEM,
        compiler_params=params(16),
    )(*parts, info)


def couple_kernel(place, a, b, c, d, weight, out):
    parts = [r[...].astype(F32) for r in (a, b, c, d)]
    rows = out.shape[0] - INFO
    probe = (parts[0] + parts[1] + parts[2] + parts[3]).astype(BF16)
    infos = [p[rows : rows + 1] for p in parts] + [jnp.zeros((INFO - RING, out.shape[1]), F32)]

    def store(side):
        inner = lax.dot_general(probe, weight[...], (((1,), (side,)), ((), ())), preferred_element_type=F32)
        out[...] = jnp.concatenate([inner[:rows]] + infos, axis=0).astype(BF16)

    @pl.when(place[KIND] == 0)
    def _():
        store(1)

    @pl.when(place[KIND] == 1)
    def _():
        store(0)


def couple(place, parts, weight):
    return pl.pallas_call(
        couple_kernel,
        out_shape=jax.ShapeDtypeStruct(parts[0].shape, BF16),
        in_specs=[SMEM] + [VMEM] * 5,
        out_specs=VMEM,
        compiler_params=params(16),
    )(place, *parts, weight)


def expand_kernel(kind, own, place, *refs):
    held, (basis, probes, leaf), rest = refs[:RING], refs[RING : RING + 3], refs[RING + 3 :]
    out, lhs = rest[-2:]
    if own and kind == 0:
        out, seen, lhs = rest[-3:]
        for j in range(RING):
            for m in range(RING):
                seen[j, m] = held[j][m, -2 * INFO :, :BLK]
    child = place[CORE if own else OTHER]
    a_me, b_me = (place[FIRST], place[SECOND]) if own else (place[SECOND], place[FIRST])
    for j in range(RING):
        a = lax.rem(a_me + RING - j, RING)

        @pl.when(a // 2 == kind)
        def _():
            for m in range(RING):
                lhs[lax.rem(a, 2), lax.rem(b_me + RING - m, RING)] = held[j][m]

    rows = lhs.shape[2] - INFO
    rank = lhs.shape[3]
    _, count, size, _ = leaf.shape
    done = []
    for t in range(count):
        at = slice(t * size, (t + 1) * size)
        low = lax.dot_general(
            lhs[...].reshape(-1, rank), basis[at], (((1,), (1,)), ((), ())), preferred_element_type=F32
        )
        low = jnp.concatenate([low[i : i + rows] for i in range(0, low.shape[0], rows + INFO)], axis=0)
        near = lax.dot_general(
            probes[child, :, at], leaf[child, t], (((1,), (1 - kind,)), ((), ())), preferred_element_type=F32
        )
        done.append(low + near)
    done = jnp.concatenate(done, axis=1).reshape(done[0].shape[0], -1, BLK)
    if not own:
        done = jnp.concatenate([rest[0][...].astype(F32), done], axis=1)
    out[...] = done.astype(BF16)


def expand(kind, place, held, basis, probes, leaf_blocks, before=None):
    local, rank = basis.shape
    samples = probes.shape[1]
    own = before is None
    blocks = local // BLK * (1 if own else 2)
    rest = [] if own else [before]
    shapes = [jax.ShapeDtypeStruct((samples, blocks, BLK), BF16)]
    if own and kind == 0:
        shapes.append(jax.ShapeDtypeStruct((RING, RING, 2 * INFO, BLK), BF16))
    got = pl.pallas_call(
        functools.partial(expand_kernel, kind, own),
        in_specs=[SMEM] + [VMEM] * (RING + 3 + len(rest)),
        out_specs=[VMEM] * len(shapes),
        scratch_shapes=[pltpu.VMEM((2, RING) + held[0].shape[1:], BF16)],
        out_shape=shapes,
        compiler_params=params(24),
        cost_estimate=cost(2 * samples * local * (rank + 256), 6 * 2**20),
    )(place, *held, basis, probes, leaf_blocks, *rest)
    return got if len(got) > 1 else got[0]


GROUP = 10


def send_kernel(selector, columns, *outs):
    _, share, capacity, _ = outs[0].shape
    blocks = selector.shape[1]
    for s in range(0, share, 2):
        pair = jnp.concatenate([columns[:, s + i].reshape(blocks, BLK) for i in range(2)], axis=1)
        moved = jnp.dot(selector[...], pair, preferred_element_type=F32).astype(BF16)
        for i in range(2 * RING):
            for h in range(2):
                outs[i % RING][i // RING, s + h] = moved[
                    i * capacity : (i + 1) * capacity, h * BLK : (h + 1) * BLK
                ]


def send(selector, columns, capacity):
    cols, share, near, _ = columns.shape
    return pl.pallas_call(
        send_kernel,
        grid=(share // GROUP,),
        out_shape=[jax.ShapeDtypeStruct((2, share, capacity, BLK), BF16)] * RING,
        in_specs=[
            pl.BlockSpec(selector.shape, lambda g: (0, 0)),
            pl.BlockSpec((cols, GROUP, near, BLK), lambda g: (0, g, 0, 0)),
        ],
        out_specs=[pl.BlockSpec((2, GROUP, capacity, BLK), lambda g: (0, g, 0, 0))] * RING,
        compiler_params=params(32),
        cost_estimate=cost(2 * selector.size * share * BLK, 8 * 2**20),
    )(selector, columns)


def place_kernel(placer, *refs):
    parts, out = refs[:-1], refs[-1]
    for s in range(0, out.shape[0], 2):
        arrived = jnp.concatenate(
            [jnp.concatenate([part[0, s], part[0, s + 1]], axis=1) for part in parts], axis=0
        )
        got = jnp.dot(placer[...], arrived, preferred_element_type=F32)
        out[s] = got[:, :BLK]
        out[s + 1] = got[:, BLK:]


def place_blocks(placer, near):
    far = [swap_core(p) for p in near]
    _, share, capacity, _ = near[0].shape
    spec = lambda half: pl.BlockSpec((1, GROUP, capacity, BLK), lambda g: (half, g, 0, 0))
    return pl.pallas_call(
        place_kernel,
        grid=(share // GROUP,),
        out_shape=jax.ShapeDtypeStruct((share, placer.shape[0], BLK), F32),
        in_specs=[pl.BlockSpec(placer.shape, lambda g: (0, 0))] + [spec(0)] * RING + [spec(1)] * RING,
        out_specs=pl.BlockSpec((GROUP, placer.shape[0], BLK), lambda g: (g, 0, 0)),
        compiler_params=params(32),
        cost_estimate=cost(2 * placer.size * share * BLK, 10 * 2**20),
    )(placer, *near, *far).transpose(1, 0, 2)


def whole(*values):
    return jnp.stack(values).astype(jnp.int32)


def per_device(omega, u_basis, v_basis, coupling, leaf_blocks, child_map):
    y_me, core, z_me, x_me = (lax.axis_index(a) for a in ALL)
    samples = omega.shape[0]
    rank = u_basis.shape[2]
    rows = 2 * samples
    row_count, col_count = 2 * RING, RING * RING
    near = child_map.size
    owner_rows = near * col_count
    capacity = 2 * owner_rows // row_count
    share = samples // col_count
    a_me = jnp.where(core == 0, x_me, z_me)
    b_me = jnp.where(core == 0, z_me, x_me)

    mine = jnp.where(core == 0, child_map, child_map[::-1]).reshape(-1)
    mine = jnp.concatenate([mine // owner_rows, mine % owner_rows]).astype(F32)
    both = jnp.concatenate([mine, swap_core(mine)])
    info = jnp.zeros((INFO, rank), F32).at[0, : both.size].set(both)

    spot = whole(core, 1 - core, a_me, b_me, a_me // 2)
    probes = omega.transpose(1, 0, 2)
    own, got = [], []
    for basis in (v_basis, u_basis):
        both_parts = jnp.einsum("scn,cnr->csr", omega, basis, preferred_element_type=F32).astype(BF16)
        own.append(lax.dynamic_index_in_dim(both_parts, core, 0, keepdims=False))
        got.append(swap_core(lax.dynamic_index_in_dim(both_parts, 1 - core, 0, keepdims=False)))
    pieces = merge(spot, *own, *got)
    coupling, u_late, pieces = lax.optimization_barrier((coupling, u_basis, pieces))
    weight = lax.dynamic_index_in_dim(coupling, core, 0, keepdims=False)
    u_own = lax.dynamic_index_in_dim(u_late, core, 0, keepdims=False)
    pieces = [pieces[0]] + [ring_zx(pieces[k], True, k) for k in STEPS]
    pieces = sum_split(spot, pieces)
    pieces = [pieces[0]] + [ring_zx(pieces[k], False, k) for k in STEPS]
    piece = sum_info(pieces, info)
    u_own, probes, piece, u_late = lax.optimization_barrier((u_own, probes, piece, u_late))
    u_other = lax.dynamic_index_in_dim(u_late, 1 - core, 0, keepdims=False)
    inner = couple(spot, [piece] + [ring_y(piece, k) for k in (1, 2, 3)], weight)
    inner = jnp.stack([inner] + [ring_zx(inner, False, k) for k in (1, 2, 3)])
    u_other, inner = lax.optimization_barrier((u_other, inner))
    held = [inner] + [ring_zx(inner, True, k) for k in (1, 2, 3)]
    swapped = [swap_core(p) for p in held]

    first, seen = expand(0, spot, held, u_own, probes, leaf_blocks)
    y_samp = expand(0, spot, swapped, u_other, probes, leaf_blocks, first)
    seen, y_samp, v_late, count = lax.optimization_barrier((seen, y_samp, v_basis, jnp.arange(owner_rows)))
    v_parts = [lax.dynamic_index_in_dim(v_late, c, 0, keepdims=False) for c in (core, 1 - core)]
    first = expand(1, spot, held, v_parts[0], probes, leaf_blocks)
    z_samp = expand(1, spot, swapped, v_parts[1], probes, leaf_blocks, first)

    fields = both.size
    seen = seen[:, :, INFO : INFO + RING, :fields]
    at = jnp.arange(RING)
    z_step, x_step = (z_me - at) % RING, (x_me - at) % RING
    flat = jnp.where(
        core == 0, x_step[None, :] * RING + z_step[:, None], z_step[:, None] * RING + x_step[None, :]
    ).reshape(-1)
    seen = seen.reshape(col_count, RING, 2, 2, near)[flat].astype(jnp.int32)
    seen = seen.transpose(3, 2, 1, 0, 4).reshape(2, row_count, owner_rows)
    dest, home = seen[0], seen[1]
    same = (dest[:, :, None] == dest[:, None, :]).astype(jnp.int32)
    before = (count[None, :] < count[:, None]).astype(jnp.int32)
    order = jnp.sum(same * before[None], axis=2)

    step = (dest[0] // 2 - y_me) % RING
    slot = (jnp.where(dest[0] % 2 == core, 0, RING) + step) * capacity + order[0]
    selector = (jnp.arange(row_count * capacity)[:, None] == slot[None, :]).astype(BF16)
    def columns(samp):
        got = lax.all_to_all(samp, ("z", "x"), split_axis=0, concat_axis=0, tiled=True)
        return got.reshape(col_count, share, near, BLK)

    y_cols = columns(y_samp)
    z_samp, y_cols = lax.optimization_barrier((z_samp, y_cols))
    y_out = send(selector, y_cols, capacity)
    y_out = [y_out[0]] + [ring_y(y_out[k], k) for k in (1, 2, 3)]
    z_out = list(send(selector, columns(z_samp), capacity))
    order, home, z_out[0] = lax.optimization_barrier((order, home, z_out[0]))
    arriving = jnp.where(dest == y_me * 2 + core, order, -1)
    spots = jnp.arange(capacity)
    ids = jnp.sum((spots[None, :, None] == arriving[:, None, :]) * (home + 1)[:, None, :], axis=2) - 1
    placer = (jnp.arange(owner_rows)[:, None] == ids.reshape(-1)[None, :]).astype(BF16)

    parent_y = place_blocks(placer, y_out)
    z_out[2], parent_y = lax.optimization_barrier((z_out[2], parent_y))
    z_out = [z_out[0]] + [ring_y(z_out[k], k) for k in (1, 2, 3)]
    return parent_y, place_blocks(placer, z_out)


def solution(mesh):
    fine = Mesh(mesh.devices.reshape(RING, 2, RING, RING), ALL)
    return jax.shard_map(
        per_device,
        mesh=fine,
        in_specs=(
            P(None, None, ALL),
            P(None, ALL, None),
            P(None, ALL, None),
            P(),
            P(None, ALL, None, None),
            P(None, ALL),
        ),
        out_specs=(P(("y", "core"), ("z", "x"), None), P(("y", "core"), ("z", "x"), None)),
        check_vma=False,
    )
```

```python
import functools

import jax
import jax.numpy as jnp
from jax import lax
from jax.experimental import pallas as pl
from jax.experimental.pallas import tpu as pltpu
from jax.sharding import Mesh, PartitionSpec as P

BLK = 128
ALL = ("y", "core", "z", "x")
RING = 4
STEPS = (1, 3, 2)
INFO = 8
BF16, F32 = jnp.bfloat16, jnp.float32


def ring_y(x, step):
    return lax.ppermute(x, "y", [(i, (i + step) % RING) for i in range(RING)])


def swap_core(x):
    return lax.ppermute(x, "core", [(0, 1), (1, 0)])


def ring_zx(x, first, step):
    pairs = []
    for core in range(2):
        for zz in range(RING):
            for xx in range(RING):
                along_x = (core == 0) == first
                to_z = zz if along_x else (zz + step) % RING
                to_x = (xx + step) % RING if along_x else xx
                pairs.append(((core * RING + zz) * RING + xx, (core * RING + to_z) * RING + to_x))
    return lax.ppermute(x, ("core", "z", "x"), pairs)


VMEM = pl.BlockSpec(memory_space=pltpu.VMEM)
SMEM = pl.BlockSpec(memory_space=pltpu.SMEM)
HBM = pl.BlockSpec(memory_space=pltpu.HBM)
ANY = pl.BlockSpec(memory_space=pl.ANY)


def cost(flops, moved):
    return pl.CostEstimate(flops=flops, bytes_accessed=moved, transcendentals=0)


def params(mib):
    return pltpu.CompilerParams(vmem_limit_bytes=mib * 2**20)


CORE, OTHER, FIRST, SECOND, KIND = range(5)


def merge_kernel(place, v, u, v_got, u_got, *outs):
    rows = outs[0].shape[0]
    for k, out in enumerate(outs):
        part = lax.rem(place[FIRST] + k, RING)
        at = pl.ds(pl.multiple_of(lax.rem(part, 2) * rows, rows), rows)

        @pl.when(part < 2)
        def _():
            out[...] = (v[at].astype(F32) + v_got[at].astype(F32)).astype(BF16)

        @pl.when(part >= 2)
        def _():
            out[...] = (u[at].astype(F32) + u_got[at].astype(F32)).astype(BF16)


def merge(place, v, u, v_got, u_got):
    samples, rank = v.shape
    return pl.pallas_call(
        merge_kernel,
        out_shape=[jax.ShapeDtypeStruct((samples // 2, rank), BF16)] * RING,
        in_specs=[SMEM] + [VMEM] * 4,
        out_specs=[VMEM] * RING,
        compiler_params=params(16),
    )(place, v, u, v_got, u_got)


def sum_split_kernel(place, *refs):
    ins, outs = refs[:RING], refs[RING:]
    for k in range(RING):
        at = lax.rem(place[SECOND] + k, RING)
        total = ins[0][at].astype(F32)
        for part in ins[1:]:
            total = total + part[at].astype(F32)
        outs[k][...] = total.astype(BF16)


def sum_split(place, parts):
    parts = [p.reshape(RING, -1, p.shape[-1]) for p in parts]
    return pl.pallas_call(
        sum_split_kernel,
        out_shape=[jax.ShapeDtypeStruct(parts[0].shape[1:], BF16)] * RING,
        in_specs=[SMEM] + [VMEM] * RING,
        out_specs=[VMEM] * RING,
        compiler_params=params(16),
    )(place, *parts)


def sum_info_kernel(a, b, c, d, info, out):
    total = a[...].astype(F32) + b[...].astype(F32) + c[...].astype(F32) + d[...].astype(F32)
    out[...] = jnp.concatenate([total, info[...]], axis=0).astype(BF16)


def sum_info(parts, info):
    rows, rank = parts[0].shape
    return pl.pallas_call(
        sum_info_kernel,
        out_shape=jax.ShapeDtypeStruct((rows + INFO, rank), BF16),
        in_specs=[VMEM] * 5,
        out_specs=VMEM,
        compiler_params=params(16),
    )(*parts, info)


def couple_kernel(place, a, b, c, d, weight, out):
    parts = [r[...].astype(F32) for r in (a, b, c, d)]
    rows = out.shape[0] - INFO
    probe = (parts[0] + parts[1] + parts[2] + parts[3]).astype(BF16)
    infos = [p[rows : rows + 1] for p in parts] + [jnp.zeros((INFO - RING, out.shape[1]), F32)]

    def store(side):
        inner = lax.dot_general(probe, weight[...], (((1,), (side,)), ((), ())), preferred_element_type=F32)
        out[...] = jnp.concatenate([inner[:rows]] + infos, axis=0).astype(BF16)

    @pl.when(place[KIND] == 0)
    def _():
        store(1)

    @pl.when(place[KIND] == 1)
    def _():
        store(0)


def couple(place, parts, weight):
    return pl.pallas_call(
        couple_kernel,
        out_shape=jax.ShapeDtypeStruct(parts[0].shape, BF16),
        in_specs=[SMEM] + [VMEM] * 5,
        out_specs=VMEM,
        compiler_params=params(16),
    )(place, *parts, weight)


def expand_kernel(kind, own, place, *refs):
    held, (basis, probes, leaf), rest = refs[:RING], refs[RING : RING + 3], refs[RING + 3 :]
    out, lhs = rest[-2:]
    if own and kind == 0:
        out, seen, lhs = rest[-3:]
        for j in range(RING):
            for m in range(RING):
                seen[j, m] = held[j][m, -2 * INFO :, :BLK]
    child = place[CORE if own else OTHER]
    a_me, b_me = (place[FIRST], place[SECOND]) if own else (place[SECOND], place[FIRST])
    for j in range(RING):
        a = lax.rem(a_me + RING - j, RING)

        @pl.when(a // 2 == kind)
        def _():
            for m in range(RING):
                lhs[lax.rem(a, 2), lax.rem(b_me + RING - m, RING)] = held[j][m]

    rows = lhs.shape[2] - INFO
    rank = lhs.shape[3]
    _, count, size, _ = leaf.shape
    done = []
    for t in range(count):
        at = slice(t * size, (t + 1) * size)
        low = lax.dot_general(
            lhs[...].reshape(-1, rank), basis[at], (((1,), (1,)), ((), ())), preferred_element_type=F32
        )
        low = jnp.concatenate([low[i : i + rows] for i in range(0, low.shape[0], rows + INFO)], axis=0)
        near = lax.dot_general(
            probes[child, :, at], leaf[child, t], (((1,), (1 - kind,)), ((), ())), preferred_element_type=F32
        )
        done.append(low + near)
    done = jnp.concatenate(done, axis=1).reshape(done[0].shape[0], -1, BLK)
    if not own:
        done = jnp.concatenate([rest[0][...].astype(F32), done], axis=1)
    out[...] = done.astype(BF16)


def expand(kind, place, held, basis, probes, leaf_blocks, before=None):
    local, rank = basis.shape
    samples = probes.shape[1]
    own = before is None
    blocks = local // BLK * (1 if own else 2)
    rest = [] if own else [before]
    shapes = [jax.ShapeDtypeStruct((samples, blocks, BLK), BF16)]
    if own and kind == 0:
        shapes.append(jax.ShapeDtypeStruct((RING, RING, 2 * INFO, BLK), BF16))
    got = pl.pallas_call(
        functools.partial(expand_kernel, kind, own),
        in_specs=[SMEM] + [VMEM] * (RING + 3 + len(rest)),
        out_specs=[VMEM] * len(shapes),
        scratch_shapes=[pltpu.VMEM((2, RING) + held[0].shape[1:], BF16)],
        out_shape=shapes,
        compiler_params=params(24),
        cost_estimate=cost(2 * samples * local * (rank + 256), 6 * 2**20),
    )(place, *held, basis, probes, leaf_blocks, *rest)
    return got if len(got) > 1 else got[0]


GROUP = 10


def send_kernel(selector, columns, *outs):
    _, share, capacity, _ = outs[0].shape
    blocks = selector.shape[1]
    for s in range(0, share, 2):
        pair = jnp.concatenate([columns[:, s + i].reshape(blocks, BLK) for i in range(2)], axis=1)
        moved = jnp.dot(selector[...], pair, preferred_element_type=F32).astype(BF16)
        for i in range(2 * RING):
            for h in range(2):
                outs[i % RING][i // RING, s + h] = moved[
                    i * capacity : (i + 1) * capacity, h * BLK : (h + 1) * BLK
                ]


def send(selector, columns, capacity):
    cols, share, near, _ = columns.shape
    return pl.pallas_call(
        send_kernel,
        grid=(share // GROUP,),
        out_shape=[jax.ShapeDtypeStruct((2, share, capacity, BLK), BF16)] * RING,
        in_specs=[
            pl.BlockSpec(selector.shape, lambda g: (0, 0)),
            pl.BlockSpec((cols, GROUP, near, BLK), lambda g: (0, g, 0, 0)),
        ],
        out_specs=[pl.BlockSpec((2, GROUP, capacity, BLK), lambda g: (0, g, 0, 0))] * RING,
        compiler_params=params(32),
        cost_estimate=cost(2 * selector.size * share * BLK, 8 * 2**20),
    )(selector, columns)


def place_kernel(placer, *refs):
    parts, out = refs[:-1], refs[-1]
    for s in range(0, out.shape[0], 2):
        arrived = jnp.concatenate(
            [jnp.concatenate([part[0, s], part[0, s + 1]], axis=1) for part in parts], axis=0
        )
        got = jnp.dot(placer[...], arrived, preferred_element_type=F32)
        out[s] = got[:, :BLK]
        out[s + 1] = got[:, BLK:]


def place_blocks(placer, near):
    far = [swap_core(p) for p in near]
    _, share, capacity, _ = near[0].shape
    spec = lambda half: pl.BlockSpec((1, GROUP, capacity, BLK), lambda g: (half, g, 0, 0))
    return pl.pallas_call(
        place_kernel,
        grid=(share // GROUP,),
        out_shape=jax.ShapeDtypeStruct((share, placer.shape[0], BLK), F32),
        in_specs=[pl.BlockSpec(placer.shape, lambda g: (0, 0))] + [spec(0)] * RING + [spec(1)] * RING,
        out_specs=pl.BlockSpec((GROUP, placer.shape[0], BLK), lambda g: (g, 0, 0)),
        compiler_params=params(32),
        cost_estimate=cost(2 * placer.size * share * BLK, 10 * 2**20),
    )(placer, *near, *far).transpose(1, 0, 2)


def whole(*values):
    return jnp.stack(values).astype(jnp.int32)


def per_device(omega, u_basis, v_basis, coupling, leaf_blocks, child_map):
    y_me, core, z_me, x_me = (lax.axis_index(a) for a in ALL)
    samples = omega.shape[0]
    rank = u_basis.shape[2]
    rows = 2 * samples
    row_count, col_count = 2 * RING, RING * RING
    near = child_map.size
    owner_rows = near * col_count
    capacity = 2 * owner_rows // row_count
    share = samples // col_count
    a_me = jnp.where(core == 0, x_me, z_me)
    b_me = jnp.where(core == 0, z_me, x_me)

    mine = jnp.where(core == 0, child_map, child_map[::-1]).reshape(-1)
    mine = jnp.concatenate([mine // owner_rows, mine % owner_rows]).astype(F32)
    both = jnp.concatenate([mine, swap_core(mine)])
    info = jnp.zeros((INFO, rank), F32).at[0, : both.size].set(both)

    spot = whole(core, 1 - core, a_me, b_me, a_me // 2)
    probes = omega.transpose(1, 0, 2)
    own, got = [], []
    for basis in (v_basis, u_basis):
        both_parts = jnp.einsum("scn,cnr->csr", omega, basis, preferred_element_type=F32).astype(BF16)
        own.append(lax.dynamic_index_in_dim(both_parts, core, 0, keepdims=False))
        got.append(swap_core(lax.dynamic_index_in_dim(both_parts, 1 - core, 0, keepdims=False)))
    pieces = merge(spot, *own, *got)
    coupling, u_late, pieces = lax.optimization_barrier((coupling, u_basis, pieces))
    weight = lax.dynamic_index_in_dim(coupling, core, 0, keepdims=False)
    u_own = lax.dynamic_index_in_dim(u_late, core, 0, keepdims=False)
    pieces = [pieces[0]] + [ring_zx(pieces[k], True, k) for k in STEPS]
    pieces = sum_split(spot, pieces)
    pieces = [pieces[0]] + [ring_zx(pieces[k], False, k) for k in STEPS]
    piece = sum_info(pieces, info)
    u_own, probes, piece, u_late = lax.optimization_barrier((u_own, probes, piece, u_late))
    u_other = lax.dynamic_index_in_dim(u_late, 1 - core, 0, keepdims=False)
    inner = couple(spot, [piece] + [ring_y(piece, k) for k in (1, 2, 3)], weight)
    inner = jnp.stack([inner] + [ring_zx(inner, False, k) for k in (1, 2, 3)])
    u_other, inner = lax.optimization_barrier((u_other, inner))
    held = [inner] + [ring_zx(inner, True, k) for k in (1, 2, 3)]
    swapped = [swap_core(p) for p in held]

    first, seen = expand(0, spot, held, u_own, probes, leaf_blocks)
    y_samp = expand(0, spot, swapped, u_other, probes, leaf_blocks, first)
    seen, y_samp, v_late, count = lax.optimization_barrier((seen, y_samp, v_basis, jnp.arange(owner_rows)))
    v_parts = [lax.dynamic_index_in_dim(v_late, c, 0, keepdims=False) for c in (core, 1 - core)]
    first = expand(1, spot, held, v_parts[0], probes, leaf_blocks)
    z_samp = expand(1, spot, swapped, v_parts[1], probes, leaf_blocks, first)

    fields = both.size
    seen = seen[:, :, INFO : INFO + RING, :fields]
    at = jnp.arange(RING)
    z_step, x_step = (z_me - at) % RING, (x_me - at) % RING
    flat = jnp.where(
        core == 0, x_step[None, :] * RING + z_step[:, None], z_step[:, None] * RING + x_step[None, :]
    ).reshape(-1)
    seen = seen.reshape(col_count, RING, 2, 2, near)[flat].astype(jnp.int32)
    seen = seen.transpose(3, 2, 1, 0, 4).reshape(2, row_count, owner_rows)
    dest, home = seen[0], seen[1]
    same = (dest[:, :, None] == dest[:, None, :]).astype(jnp.int32)
    before = (count[None, :] < count[:, None]).astype(jnp.int32)
    order = jnp.sum(same * before[None], axis=2)

    step = (dest[0] // 2 - y_me) % RING
    slot = (jnp.where(dest[0] % 2 == core, 0, RING) + step) * capacity + order[0]
    selector = (jnp.arange(row_count * capacity)[:, None] == slot[None, :]).astype(BF16)
    arriving = jnp.where(dest == y_me * 2 + core, order, -1)
    spots = jnp.arange(capacity)
    ids = jnp.sum((spots[None, :, None] == arriving[:, None, :]) * (home + 1)[:, None, :], axis=2) - 1
    placer = (jnp.arange(owner_rows)[:, None] == ids.reshape(-1)[None, :]).astype(BF16)

    def columns(samp):
        got = lax.all_to_all(samp, ("z", "x"), split_axis=0, concat_axis=0, tiled=True)
        return got.reshape(col_count, share, near, BLK)

    y_cols = columns(y_samp)
    y_out = send(selector, y_cols, capacity)
    y_out = [y_out[0]] + [ring_y(y_out[k], k) for k in (1, 2, 3)]
    z_out = list(send(selector, columns(z_samp), capacity))
    parent_y = place_blocks(placer, y_out)
    z_out[2], parent_y = lax.optimization_barrier((z_out[2], parent_y))
    z_out = [z_out[0]] + [ring_y(z_out[k], k) for k in (1, 2, 3)]
    return parent_y, place_blocks(placer, z_out)


def solution(mesh):
    fine = Mesh(mesh.devices.reshape(RING, 2, RING, RING), ALL)
    return jax.shard_map(
        per_device,
        mesh=fine,
        in_specs=(
            P(None, None, ALL),
            P(None, ALL, None),
            P(None, ALL, None),
            P(),
            P(None, ALL, None, None),
            P(None, ALL),
        ),
        out_specs=(P(("y", "core"), ("z", "x"), None), P(("y", "core"), ("z", "x"), None)),
        check_vma=False,
    )
```
